768 devices in a mesh: rep: 12 (over x, z_lo), shard: 64 (over z_hi, y, core).
Axes of the slice: x: 4, y: 8, z: 12 (z_hi: 4, z_lo: 3; z = z_hi * 3 + z_lo), core: 2. Of those that a mesh axis runs over, the one named last changes fastest.
Arguments:
- pooled: bfloat16 [98304, 1024], P(('rep', 'shard')), may hold values from -6 to 6
- layer_grad: bfloat16 [98304, 512], P(('rep', 'shard')), may hold values from -6 to 6
- dense_weight: bfloat16 [1024, 512], replicated, may hold values from -0.25 to 0.25
- bag_owner: int32 [1572864, 1], P(('rep', 'shard')), may hold values from 0 to 63; in each aligned block of 2048 rows (0 to 2047, 2048 to 4095, ...) at most 64 rows name the same one
- bag_slot: int32 [1572864], P(('rep', 'shard')), may hold values from 0 to 1535
- touched: int32 [98304], P('shard'), may hold values from 0 to 4095, as said below
- codes: bfloat16 [262144, 256], P('shard'), may hold values from 0 to 255, as said below
- row_scale: float32 [262144], P('shard'), may hold values from 0.002 to 0.02
- row_bias: float32 [262144], P('shard'), may hold values from -1 to 1
- accum: float32 [262144], P('shard'), may hold values from 1 to 100
Outputs:
- weight_grad: float32 [1024, 512], replicated
- new_codes: float32 [98304, 256], P('shard')
- new_scale: float32 [98304], P('shard')
- new_bias: float32 [98304], P('shard')
- new_accum: float32 [98304], P('shard')
The draws below stay inside these ranges and needn't reach their ends.
Inputs may be any that keep to these rules, and one draw needn't show every extreme that they name: `bag_owner`: within the lookups of one device no shard is named more than 64 times. `touched`: each aligned block of 1536 entries lists distinct local rows of one shard, in shard order. `codes`: whole numbers.
All inputs are finite; a program needn't handle non-finite values.
Results may differ from the reference program's by a relative error of at most 0.00047.
Values may be sent and summed in bfloat16 or wider, within the bound.
No kernel may reach another device: no remote copies, remote signals or barrier semaphores. Data moves between devices by JAX's collectives and lax.ppermute only.
A program may use at most 32 MiB of HBM per device.

```python
import math
import jax
import jax.numpy as jnp
import numpy as np
from jax import lax

E = 256
H = 512
F = 4
L = 4
B_DEV = 128
TOUCH = 1536
ROWS_DEV = 4096
TOKENS = 98304
ENT_DEV = 2048
ENTRIES = 1572864
CAP = 64
ROWS = 262144
N_REP = 12
N_SHARD = 64


def draw_touched(key, part):
    key = jax.random.fold_in(key, 2)
    shard_keys = jax.random.split(key, N_SHARD)
    lists = jax.vmap(lambda one: jax.random.permutation(one, ROWS_DEV)[:TOUCH])(shard_keys)
    return lists.reshape(-1).astype(jnp.int32)


def draw_codes(key, part):
    key = jax.random.fold_in(key, 3)
    values = jax.random.uniform(key, (ROWS, E), jnp.float32, 0.0, 256.0)
    return jnp.minimum(jnp.floor(values), 255.0).astype(jnp.bfloat16)


def set_ends(array, key, least, top_value):
    dims = array.shape
    index_at = [jax.random.randint(jax.random.fold_in(key, axis), (), 0, dims[axis]) for axis in range(len(dims))]
    array = array.at[tuple(index_at)].set(least)
    longest = dims.index(max(dims))
    index_at[longest] = (index_at[longest] + 1) % dims[longest]
    return array.at[tuple(index_at)].set(top_value)


def level_of(own_key, shape, cuts, smallest, high):
    gain, own = 1.0, jax.random.fold_in(own_key, 6)
    for axis_at, parts in cuts:
        heights = jnp.exp(jax.random.uniform(jax.random.fold_in(own, axis_at), (parts,), jnp.float32, smallest / len(cuts), high / len(cuts)))
        gain = gain * jnp.repeat(heights, shape[axis_at] // parts).reshape([-1 if axis == axis_at else 1 for axis in range(len(shape))])
    return gain


def rank_table(amount, slope):
    portions = [(1 << 20) // math.isqrt(grade ** slope) + 1 for grade in range(1, amount + 1)]
    scale = 1 + sum(portions) // (1 << 30)
    return np.cumsum(np.array([max(1, weight // scale) for weight in portions]))


def ranked(rng, dims, number_of, slope):
    grid = rank_table(number_of, slope)
    ticket = jax.random.randint(jax.random.fold_in(rng, 1), dims, 0, int(grid[number_of - 1]))
    standing = jnp.searchsorted(jnp.asarray(grid, jnp.int32), ticket, side="right")
    return jax.random.permutation(jax.random.fold_in(rng, 2), number_of)[standing].astype(jnp.int32)


def shared_out(stream_key, own, number, rows, number_of, top, most, slope):
    sequence = jax.random.permutation(stream_key, number_of)
    heavy_load, common = load_shares(number_of, rows * top, most, slope, True), load_shares(number_of, rows * top, most, slope, False)
    places = jnp.arange(number_of)

    def named(sizes, offset_by):
        used = int((sizes > 0).sum())
        fixed = max(1, used // 4)
        moved = fixed + (places - fixed + offset_by * (used - fixed)) % max(1, number_of - fixed)
        return jnp.zeros((number_of,), jnp.int32).at[sequence[jnp.where(places < fixed, places, moved)]].set(jnp.asarray(sizes, jnp.int32))

    sizes = jnp.where(number % 4 == 0, named(heavy_load, number // 4), named(common, number - number // 4 - 1))
    mixed = jax.random.permutation(jax.random.fold_in(own, 3), number_of)
    donor, receiver = mixed[0:number_of // 2 * 2:2], mixed[1:number_of // 2 * 2:2]
    slack = jnp.minimum(sizes[donor] - 1, most - sizes[receiver]) // 2
    slack = jnp.where((donor == sequence[0]) | (receiver == sequence[0]) | (sizes[receiver] == 0), 0, jnp.maximum(slack, 0))
    moved = jax.random.randint(jax.random.fold_in(own, 4), (number_of // 2,), 0, 1 << 20) % (slack + 1)
    sizes = sizes.at[donor].add(-moved).at[receiver].add(moved)
    items = jnp.searchsorted(jnp.cumsum(sizes), jnp.arange(rows * top), side="right").astype(jnp.int32)
    table = items.reshape(top, rows).T
    table = table[jax.random.permutation(jax.random.fold_in(own, 1), rows)]
    offset_by = jax.random.randint(jax.random.fold_in(own, 2), (rows, 1), 0, top)
    return jnp.take_along_axis(table, (jnp.arange(top)[None, :] + offset_by) % top, axis=1)


def load_shares(amount, total, reach, slope, full):
    weights = [(1 << 20) // math.isqrt(rank ** slope) + 1 for rank in range(1, amount + 1)]
    largest = reach if full else min(reach, max(-(-total // amount), total * weights[0] // sum(weights)))
    least = 1 if total - largest >= amount - 1 else 0
    given, spare = [largest] + [least] * (amount - 1), total - largest - least * (amount - 1)
    while spare > 0:
        movable = [i for i in range(1, amount) if given[i] < largest] or [i for i in range(1, amount) if given[i] < reach]
        mass, budget = sum([weights[i] for i in movable]), spare
        for i in movable:
            extra = min(reach - given[i], max(1, budget * weights[i] // mass), spare)
            given[i] = given[i] + extra
            spare = spare - extra
    return np.array(given)


def normal_values(stream_key, extent, scale, most, cuts=(), kind=jnp.bfloat16):
    factor_of = level_of(stream_key, extent, cuts, -0.22, 0.18) if cuts else 1.0
    drawn = jax.random.normal(stream_key, extent, jnp.float32) * scale * factor_of
    return jnp.minimum(jnp.maximum(drawn, -most), most).astype(kind)


def setup_inputs(seed: int = 0) -> dict:
    arg_keys = jax.random.split(jax.random.key(seed), 11)
    pooled = normal_values(arg_keys[0], (TOKENS, F * E), 1.0, 6.0, ((0, 768),))
    layer_grad = normal_values(arg_keys[1], (TOKENS, H), 1.0, 6.0, ((0, 768),))
    dense_weight = normal_values(arg_keys[2], (F * E, H), H ** -0.5, 0.25)
    bag_owner_keys = jax.random.split(jax.random.fold_in(arg_keys[3], 1), ENTRIES // ENT_DEV)
    bag_owner_turns = jax.random.permutation(jax.random.fold_in(arg_keys[3], 3), ENTRIES // ENT_DEV)
    bag_owner = jax.vmap(lambda own, number: shared_out(jax.random.fold_in(arg_keys[3], 2), own, number, ENT_DEV, N_SHARD, 1, CAP, 1))(bag_owner_keys, bag_owner_turns).reshape((ENTRIES, 1))
    bag_slot = set_ends(ranked(arg_keys[4], (ENTRIES,), TOUCH, 2), jax.random.fold_in(arg_keys[4], 3), 0, TOUCH - 1).astype(jnp.int32)
    touched = draw_touched(jax.random.fold_in(arg_keys[10], 71), 0)
    codes = draw_codes(jax.random.fold_in(arg_keys[10], 71), 0)
    row_scale = jnp.clip(jnp.exp(math.log(0.02) - 2.30258502 * jax.random.uniform(arg_keys[7], (ROWS,), jnp.float32) ** level_of(arg_keys[7], (ROWS,), ((0, 64),), -0.2, 0.2)), 0.002, 0.02)
    row_bias = jnp.clip(jax.random.uniform(arg_keys[8], (ROWS,), jnp.float32, -1.0, 1.0) * level_of(arg_keys[8], (ROWS,), ((0, 64),), -0.4, 0.0), -1.0, 1.0)
    accum = jnp.clip(jnp.exp(math.log(100.0) - 4.6051702 * jax.random.uniform(arg_keys[9], (ROWS,), jnp.float32) ** level_of(arg_keys[9], (ROWS,), ((0, 64),), -0.2, 0.2)), 1.0, 100.0)
    return {"pooled": pooled, "layer_grad": layer_grad, "dense_weight": dense_weight, "bag_owner": bag_owner, "bag_slot": bag_slot, "touched": touched, "codes": codes, "row_scale": row_scale, "row_bias": row_bias, "accum": accum}


def reference(pooled, layer_grad, dense_weight, bag_owner, bag_slot, touched, codes, row_scale, row_bias, accum):
    weight_grad = jnp.dot(pooled.T, layer_grad, preferred_element_type=jnp.float32)
    pooled_grad = jnp.dot(layer_grad, dense_weight.T, preferred_element_type=jnp.float32).astype(jnp.bfloat16)
    blocks = N_REP * N_SHARD
    grad_rows = pooled_grad.reshape(blocks, B_DEV * F, E)
    keys = (bag_owner[:, 0] * TOUCH + bag_slot).astype(jnp.int32).reshape(blocks, ENT_DEV)

    def gather_block(total, inputs):
        rows, block_keys = inputs
        spread = jnp.repeat(rows.astype(jnp.float32), L, axis=0)
        return (total + jax.ops.segment_sum(spread, block_keys, num_segments=N_SHARD * TOUCH), None)
    row_grad, _ = lax.scan(gather_block, jnp.zeros((N_SHARD * TOUCH, E), jnp.float32), (grad_rows, keys))
    owner_of = (jnp.arange(N_SHARD * TOUCH, dtype=jnp.int32) // TOUCH).astype(jnp.int32)
    global_rows = (owner_of * ROWS_DEV + touched).astype(jnp.int32)
    weights = codes[global_rows].astype(jnp.float32) * row_scale[global_rows][:, None] + row_bias[global_rows][:, None]
    new_accum = accum[global_rows] + lax.optimization_barrier(jnp.mean(row_grad * row_grad, axis=1))
    updated = weights - 0.1 * row_grad / (jnp.sqrt(new_accum)[:, None] + 1e-06)
    lowest = lax.optimization_barrier(jnp.min(updated, axis=1))
    highest = lax.optimization_barrier(jnp.max(updated, axis=1))
    new_scale = (highest - lowest) / 255.0
    new_codes = (updated - lowest[:, None]) / new_scale[:, None]
    return (weight_grad, new_codes, new_scale, lowest, new_accum)
```

```python
import jax
import jax.numpy as jnp
from jax import lax
from jax.experimental import pallas as pl
from jax.experimental.pallas import tpu as pltpu
from jax.sharding import Mesh, PartitionSpec as P

f32, bf16, i32 = jnp.float32, jnp.bfloat16, jnp.int32
NX, NZL, NZH, NY, NC = 4, 3, 4, 8, 2
AXES = ("x", "zl", "zh", "y", "c")
REP = ("x", "zl")
SHARD = ("zh", "y", "c")
NT = (((1,), (1,)), ((), ()))


def dispatch_kernel(groups, cap, lg_ref, w_ref, owner_ref, slot_ref, rows_ref, slots_ref, g_ref):
    per_bag, bags = owner_ref.shape
    samples = lg_ref.shape[0]
    width = rows_ref.shape[1]
    lg = lg_ref[...]
    for f in range(bags // samples):
        block = lax.dot_general(lg, w_ref[f * width : (f + 1) * width, :], NT, preferred_element_type=f32)
        g_ref[f * samples : (f + 1) * samples, :] = block.astype(bf16)
    owner, slot = owner_ref[...], slot_ref[...] + 1
    group = lax.broadcasted_iota(i32, (groups, bags), 0)
    earlier = lax.broadcasted_iota(i32, (bags, bags), 0) < lax.broadcasted_iota(i32, (bags, bags), 1)
    earlier = jnp.where(earlier, 1.0, 0.0).astype(bf16)
    base = jnp.zeros((groups, 1), f32)
    packed = jnp.zeros((2 * groups, cap), f32)
    targets = []
    for j in range(per_bag):
        own = owner[j : j + 1, :]
        member = jnp.where(own == group, 1.0, 0.0)
        prefix = jnp.dot(member.astype(bf16), earlier, preferred_element_type=f32) + base
        pos = jnp.sum(member * prefix, axis=0, keepdims=True)
        base = base + jnp.sum(member, axis=1, keepdims=True)
        pos = pos.astype(i32)
        targets.append(own * cap + pos)
        place = jnp.where(pos == lax.broadcasted_iota(i32, (cap, bags), 0), 1.0, 0.0).astype(bf16)
        high = (slot[j : j + 1, :] >> 5).astype(f32)
        low = (slot[j : j + 1, :] & 31).astype(f32)
        parts = jnp.concatenate([member * high, member * low], axis=0).astype(bf16)
        packed = packed + lax.dot_general(parts, place, NT, preferred_element_type=f32)
    slots_ref[...] = (packed[:groups] * 32.0 + packed[groups:]).astype(i32) - 1
    chunk = 256
    line = lax.broadcasted_iota(i32, (chunk, bags), 0)

    def step(i, carry):
        start = pl.multiple_of(i * chunk, chunk)
        hit = (targets[0] - start) == line
        for j in range(1, per_bag):
            hit = hit | ((targets[j] - start) == line)
        pick = jnp.where(hit, 1.0, 0.0).astype(bf16)
        out = jnp.dot(pick, g_ref[...], preferred_element_type=f32)
        rows_ref[pl.ds(start, chunk), :] = out.astype(bf16)
        return carry

    lax.fori_loop(0, groups * cap // chunk, step, 0)


def dispatch(layer_grad, dense_weight, bag_owner, bag_slot, width, groups, cap):
    samples = layer_grad.shape[0]
    features = dense_weight.shape[0] // width
    bags = samples * features
    per_bag = bag_slot.shape[0] // bags

    def lay(a):
        return a.reshape(samples, features, per_bag).transpose(2, 1, 0).reshape(per_bag, bags)

    vmem = pl.BlockSpec(memory_space=pltpu.VMEM)
    return pl.pallas_call(
        lambda *refs: dispatch_kernel(groups, cap, *refs),
        out_shape=(
            jax.ShapeDtypeStruct((groups * cap, width), bf16),
            jax.ShapeDtypeStruct((groups, cap), i32),
        ),
        in_specs=[vmem] * 4,
        out_specs=(vmem, vmem),
        scratch_shapes=[pltpu.VMEM((bags, width), bf16)],
        compiler_params=pltpu.CompilerParams(vmem_limit_bytes=32 << 20),
        name="dispatch",
    )(layer_grad, dense_weight, lay(bag_owner), lay(bag_slot))


def shift(a, axis, size, k):
    return lax.ppermute(a, axis, [(i, (i + k) % size) for i in range(size)])


def scatter_sum(a, axis, size):
    me = lax.axis_index(axis)
    n = a.shape[0] // size

    def block(k):
        return lax.dynamic_slice_in_dim(a, lax.rem(me + k, size) * n, n, 0)

    got = [shift(block(k), axis, size, k) for k in range(1, size)]
    total = block(0)
    for g in got:
        total = total + g
    return total


def gather(a, axis, size):
    me = lax.axis_index(axis)
    n = a.shape[0]
    out = jnp.zeros((size * n,) + a.shape[1:], a.dtype)
    for k in range(size):
        piece = a if k == 0 else shift(a, axis, size, k)
        out = lax.dynamic_update_slice_in_dim(out, piece, lax.rem(me - k + size, size) * n, 0)
    return out


def reduce_weight(a):
    rows, columns = a.shape
    a = scatter_sum(a, "c", NC)
    a = scatter_sum(a, "x", NX)
    n = a.shape[0]
    a = a.reshape(NY, n // NY, NZH, columns // NZH).transpose(0, 2, 1, 3).reshape(NY * NZH, n // NY, columns // NZH)
    a = jnp.sum(lax.all_to_all(a, ("zh", "y"), 0, 0, tiled=True), axis=0)
    a = jnp.sum(gather(a[None], "zl", NZL), axis=0)
    a = jnp.broadcast_to(a[None], (NY * NZH,) + a.shape)
    a = lax.all_to_all(a, ("zh", "y"), 0, 0, tiled=True)
    a = a.reshape(NY, NZH, n // NY, columns // NZH).transpose(0, 2, 1, 3).reshape(n, columns)
    a = gather(a, "x", NX)
    return gather(a, "c", NC)


def shards(pooled, layer_grad, dense_weight, bag_owner, bag_slot, touched, codes, row_scale, row_bias, accum):
    groups = NZH * NY * NC
    width = codes.shape[1]
    touch = touched.shape[0]
    cap = 2 * bag_slot.shape[0] // groups
    partial_grad = lax.dot_general(pooled, layer_grad, (((0,), (0,)), ((), ())), preferred_element_type=f32)
    rows, slots = dispatch(layer_grad, dense_weight, bag_owner, bag_slot, width, groups, cap)
    slots = lax.all_to_all(slots, SHARD, 0, 0, tiled=True)
    rows = lax.all_to_all(rows.reshape(groups, cap, width), SHARD, 0, 0, tiled=True)
    weight_grad = reduce_weight(partial_grad)

    part = touch // (NX * NZL)
    mine = lax.axis_index("x") * NZL + lax.axis_index("zl")
    local = lax.dynamic_slice_in_dim(touched, mine * part, part, 0)
    old = codes[local].astype(f32) * row_scale[local][:, None] + row_bias[local][:, None]
    old_accum = accum[local]

    selector = (jnp.arange(touch, dtype=i32)[:, None] == slots.reshape(1, -1)).astype(bf16)
    total = jnp.dot(selector, rows.reshape(-1, width), preferred_element_type=f32)
    total = scatter_sum(total, "x", NX)
    total = scatter_sum(total, "zl", NZL)

    new_accum = old_accum + jnp.mean(total * total, axis=1)
    updated = old - 0.1 * total / (jnp.sqrt(new_accum)[:, None] + 1e-06)
    lowest = jnp.min(updated, axis=1)
    highest = jnp.max(updated, axis=1)
    new_scale = (highest - lowest) / 255.0
    new_codes = (updated - lowest[:, None]) / new_scale[:, None]
    small = jnp.concatenate([new_scale, lowest, new_accum, jnp.zeros((8 * width - 3 * part,), f32)])
    payload = jnp.concatenate([new_codes, small.reshape(8, width)], axis=0)
    payload = gather(gather(payload, "zl", NZL), "x", NX)
    payload = payload.reshape(NX * NZL, part + 8, width)
    new_codes = payload[:, :part].reshape(touch, width)
    small = payload[:, part:].reshape(NX * NZL, 8 * width)
    new_scale, lowest, new_accum = (small[:, i * part : (i + 1) * part].reshape(touch) for i in range(3))
    return (weight_grad, new_codes, new_scale, lowest, new_accum)


def solution(mesh):
    mesh = Mesh(mesh.devices.reshape(NX, NZL, NZH, NY, NC), AXES)
    in_specs = (
        P(AXES, None),
        P(AXES, None),
        P(),
        P(AXES, None),
        P(AXES),
        P(SHARD),
        P(SHARD, None),
        P(SHARD),
        P(SHARD),
        P(SHARD),
    )
    out_specs = (P(), P(SHARD, None), P(SHARD), P(SHARD), P(SHARD))
    return jax.shard_map(shards, mesh=mesh, in_specs=in_specs, out_specs=out_specs, check_vma=False)
```

```python
import jax
import jax.numpy as jnp
from jax import lax
from jax.experimental import pallas as pl
from jax.experimental.pallas import tpu as pltpu
from jax.sharding import Mesh, PartitionSpec as P

f32, bf16, i32 = jnp.float32, jnp.bfloat16, jnp.int32
NX, NZL, NZH, NY, NC = 4, 3, 4, 8, 2
AXES = ("x", "zl", "zh", "y", "c")
REP = ("x", "zl")
SHARD = ("zh", "y", "c")
KEYS, EXTRA = 16, 16
NT = (((1,), (1,)), ((), ()))


def dispatch_kernel(here, cap, first_ref, own_ref, prev_ref, next_ref, far_ref, w_ref, out_ref, g_ref, slots_ref, aim_ref):
    samples = own_ref.shape[0]
    depth = w_ref.shape[1]
    width = out_ref.shape[2]
    features = w_ref.shape[0] // width
    bags = samples * features
    per_bag = KEYS // features
    sources = (own_ref, prev_ref, next_ref, far_ref)
    group = lax.broadcasted_iota(i32, (here, bags), 0)
    earlier = lax.broadcasted_iota(i32, (bags, bags), 0) < lax.broadcasted_iota(i32, (bags, bags), 1)
    earlier = jnp.where(earlier, 1.0, 0.0).astype(bf16)
    lane = lax.broadcasted_iota(i32, (len(sources) * cap, bags), 0)
    packed = jnp.zeros((2 * here, len(sources) * cap), f32)
    some = 4
    line = lax.broadcasted_iota(i32, (some * cap, bags), 0)
    for q, ref in enumerate(sources):
        lg = ref[:, :depth]
        for f in range(features):
            block = lax.dot_general(lg, w_ref[f * width : (f + 1) * width, :], NT, preferred_element_type=f32)
            g_ref[f * samples : (f + 1) * samples, :] = block.astype(bf16)
        keys = jnp.transpose(ref[:, depth:].astype(f32))

        def pick(kind, j):
            at = [kind * KEYS + f * per_bag + j for f in range(features)]
            return jnp.concatenate([keys[i : i + 1, :] for i in at], axis=1)

        owners = [pick(0, j).astype(i32) - first_ref[0] for j in range(per_bag)]
        members = [jnp.where(own == group, 1.0, 0.0) for own in owners]
        stacked = jnp.concatenate(members, axis=0).astype(bf16)
        prefix = jnp.dot(stacked, earlier, preferred_element_type=f32)
        base = jnp.zeros((here, 1), f32)
        for j in range(per_bag):
            member = members[j]
            pos = jnp.sum(member * (prefix[j * here : (j + 1) * here] + base), axis=0, keepdims=True).astype(i32)
            base = base + jnp.sum(member, axis=1, keepdims=True)
            aim_ref[j : j + 1, :] = owners[j] * cap + pos
            place = jnp.where(pos + q * cap == lane, 1.0, 0.0).astype(bf16)
            parts = jnp.concatenate([member * pick(1, j), member * pick(2, j)], axis=0).astype(bf16)
            packed = packed + lax.dot_general(parts, place, NT, preferred_element_type=f32)

        def step(i, carry):
            start = i * some * cap
            aim = aim_ref[:per_bag, :] - start
            hit = aim[0:1, :] == line
            for j in range(1, per_bag):
                hit = hit | (aim[j : j + 1, :] == line)
            chosen = jnp.where(hit, 1.0, 0.0).astype(bf16)
            out = jnp.dot(chosen, g_ref[...], preferred_element_type=f32).astype(bf16)
            for k in range(some):
                out_ref[i * some + k, q * cap : (q + 1) * cap, :] = out[k * cap : (k + 1) * cap]
            return carry

        for i in range(here // some):
            step(i, 0)
    slots_ref[...] = packed
    row = lax.broadcasted_iota(i32, (EXTRA, width), 0)
    for d in range(here):
        extra = jnp.where(row == 0, slots_ref[d : d + 1, :], 0.0)
        extra = jnp.where(row == 1, slots_ref[here + d : here + d + 1, :], extra)
        out_ref[d, len(sources) * cap :, :] = extra.astype(bf16)


def vmem():
    return pl.BlockSpec(memory_space=pltpu.VMEM)


def limit():
    return pltpu.CompilerParams(vmem_limit_bytes=40 << 20)


def with_keys(layer_grad, bag_owner, bag_slot):
    samples = layer_grad.shape[0]
    slot = bag_slot.reshape(samples, KEYS) + 1
    keys = jnp.concatenate([bag_owner.reshape(samples, KEYS), slot >> 5, slot & 31], axis=1).astype(bf16)
    return jnp.concatenate([layer_grad, jnp.pad(keys, ((0, 0), (0, 128 - 3 * KEYS)))], axis=1)


def gather_near(a):
    half = a.shape[0] // 2
    prev = shift(a, "zh", NZH, 1)
    after = shift(a, "zh", NZH, NZH - 1)
    far = [shift(prev[:half], "zh", NZH, 1), shift(after[half:], "zh", NZH, NZH - 1)]
    return a, prev, after, jnp.concatenate(far, axis=0)


def dispatch(first, sources, dense_weight, width, here, cap):
    samples = sources[0].shape[0]
    features = dense_weight.shape[0] // width
    return pl.pallas_call(
        lambda *refs: dispatch_kernel(here, cap, *refs),
        out_shape=jax.ShapeDtypeStruct((here, len(sources) * cap + EXTRA, width), bf16),
        in_specs=[pl.BlockSpec(memory_space=pltpu.SMEM)] + [vmem()] * 5,
        out_specs=vmem(),
        scratch_shapes=[pltpu.VMEM((samples * features, width), bf16), pltpu.VMEM((2 * here, width), f32), pltpu.VMEM((8, samples * features), i32)],
        compiler_params=limit(),
        name="dispatch",
    )(first, *sources, dense_weight)


def collect(got, touch):
    here, height, width = got.shape
    many = height - EXTRA
    slots = got[:, many].astype(f32) * 32.0 + got[:, many + 1].astype(f32) - 1.0
    slots = jnp.pad(slots.astype(i32), ((0, 0), (0, EXTRA)), constant_values=-1)
    selector = (jnp.arange(touch, dtype=i32)[:, None] == slots.reshape(1, -1)).astype(bf16)
    return jnp.dot(selector, got.reshape(-1, width), preferred_element_type=f32)


def update_kernel(sums_ref, old_ref, accum_ref, out_ref):
    parts, part, width = sums_ref.shape
    total = sums_ref[0]
    for k in range(1, parts):
        total = total + sums_ref[k]
    new_accum = accum_ref[...] + jnp.mean(total * total, axis=1, keepdims=True)
    updated = old_ref[...] - 0.1 * total / (jnp.sqrt(new_accum) + 1e-06)
    lowest = jnp.min(updated, axis=1, keepdims=True)
    highest = jnp.max(updated, axis=1, keepdims=True)
    new_scale = (highest - lowest) / 255.0
    new_codes = (updated - lowest) / new_scale
    diagonal = lax.broadcasted_iota(i32, (part, part), 0) == lax.broadcasted_iota(i32, (part, part), 1)
    row = lax.broadcasted_iota(i32, (8, part), 0)
    small = jnp.zeros((8, part), f32)
    for i, column in enumerate((new_scale, lowest, new_accum)):
        flat = jnp.sum(jnp.where(diagonal, column, 0.0), axis=0, keepdims=True)
        small = jnp.where(row == i, flat, small)
    small = jnp.concatenate([small, jnp.zeros((8, width - part), f32)], axis=1)
    for k in range(parts):
        out_ref[k, :part, :] = new_codes
        out_ref[k, part:, :] = small


def update(sums, old, old_accum):
    parts, part, width = sums.shape
    return pl.pallas_call(
        update_kernel,
        out_shape=jax.ShapeDtypeStruct((parts, part + 8, width), f32),
        in_specs=[vmem()] * 3,
        out_specs=vmem(),
        compiler_params=limit(),
        name="update",
    )(sums, old, old_accum[:, None])


def swap(a, axis, size, bit):
    return lax.ppermute(a, axis, [(i, i ^ bit) for i in range(size)])


def halve(a, axis, size, bit, dim):
    side = (lax.axis_index(axis) & bit) // bit
    n = a.shape[dim] // 2
    keep = lax.dynamic_slice_in_dim(a, side * n, n, dim)
    send = lax.dynamic_slice_in_dim(a, (1 - side) * n, n, dim)
    return keep + swap(send, axis, size, bit)


def double(a, axis, size, bit, dim):
    other = swap(a, axis, size, bit)
    first = (lax.axis_index(axis) & bit) == 0
    return jnp.concatenate([jnp.where(first, a, other), jnp.where(first, other, a)], axis=dim)


def shift(a, axis, size, k):
    return lax.ppermute(a, axis, [(i, (i + k) % size) for i in range(size)])


def tie(*arrays):
    return lax.optimization_barrier(arrays)


def sum_over_three(a):
    me = lax.axis_index("zl")
    got = [a] + [shift(a, "zl", NZL, k) for k in range(1, NZL)]
    total = None
    for source in range(NZL):
        term = got[NZL - 1]
        for k in range(NZL - 1):
            term = jnp.where((me - k) % NZL == source, got[k], term)
        total = term if total is None else total + term
    return total


def shards(pooled, layer_grad, dense_weight, bag_owner, bag_slot, touched, codes, row_scale, row_bias, accum):
    here = NY * NC
    parts = NX * NZL
    width = codes.shape[1]
    touch = touched.shape[0]
    part = touch // parts
    cap = 2 * bag_slot.shape[0] // (NZH * here)
    first = (lax.axis_index("zh") * here).astype(i32).reshape(1)
    sources = gather_near(with_keys(layer_grad, bag_owner, bag_slot))

    w = lax.dot_general(pooled, layer_grad, (((0,), (0,)), ((), ())), preferred_element_type=f32)
    w = halve(w, "c", NC, 1, 0)
    w = halve(w, "x", NX, 1, 0)
    *sources, w = tie(*sources, w)

    rows = dispatch(first, sources, dense_weight, width, here, cap)
    got = lax.all_to_all(rows, ("y", "c"), 0, 0, tiled=True)
    w = halve(w, "x", NX, 2, 0)
    w = halve(w, "y", NY, 1, 0)
    w = halve(w, "y", NY, 2, 0)
    mine = lax.axis_index("x") * NZL + lax.axis_index("zl")
    local = lax.dynamic_slice_in_dim(touched, mine * part, part, 0)
    old = codes[local].astype(f32) * row_scale[local][:, None] + row_bias[local][:, None]
    old_accum = accum[local]
    got, w, old, old_accum = tie(got, w, old, old_accum)

    sums = collect(got, touch).reshape(parts, part, width)
    sums = lax.all_to_all(sums, REP, 0, 0, tiled=True)
    w = w + swap(w, "y", NY, 4)
    w = w + swap(w, "zh", NZH, 1)
    w = w + swap(w, "zh", NZH, 2)
    sums, w = tie(sums, w)

    payload = lax.all_to_all(update(sums, old, old_accum), REP, 0, 0, tiled=True)
    w = sum_over_three(w)
    w = double(w, "y", NY, 2, 0)
    w = double(w, "y", NY, 1, 0)
    w = double(w, "x", NX, 2, 0)
    w = double(w, "x", NX, 1, 0)
    weight_grad = double(w, "c", NC, 1, 0)
    new_codes = payload[:, :part].reshape(touch, width)
    new_scale, lowest, new_accum = (payload[:, part + i, :part].reshape(touch) for i in range(3))
    return (weight_grad, new_codes, new_scale, lowest, new_accum)


def solution(mesh):
    mesh = Mesh(mesh.devices.reshape(NX, NZL, NZH, NY, NC), AXES)
    in_specs = (
        P(AXES, None),
        P(AXES, None),
        P(),
        P(AXES, None),
        P(AXES),
        P(SHARD),
        P(SHARD, None),
        P(SHARD),
        P(SHARD),
        P(SHARD),
    )
    out_specs = (P(), P(SHARD, None), P(SHARD), P(SHARD), P(SHARD))
    return jax.shard_map(shards, mesh=mesh, in_specs=in_specs, out_specs=out_specs, check_vma=False)
```

```python
import jax
import jax.numpy as jnp
from jax import lax
from jax.experimental import pallas as pl
from jax.experimental.pallas import tpu as pltpu
from jax.sharding import Mesh, PartitionSpec as P

f32, bf16, i32 = jnp.float32, jnp.bfloat16, jnp.int32
NX, NZL, NZH, NY, NC = 4, 3, 4, 8, 2
AXES = ("x", "zl", "zh", "y", "c")
REP = ("x", "zl")
SHARD = ("zh", "y", "c")
KEYS, EXTRA = 16, 16
NT = (((1,), (1,)), ((), ()))


def dispatch_kernel(here, cap, first_ref, near_ref, w_ref, out_ref, g_ref, slots_ref, aim_ref):
    count, samples = near_ref.shape[0], near_ref.shape[1]
    depth = w_ref.shape[1]
    width = out_ref.shape[2]
    features = w_ref.shape[0] // width
    bags = samples * features
    per_bag = KEYS // features
    group = lax.broadcasted_iota(i32, (here, bags), 0)
    earlier = lax.broadcasted_iota(i32, (bags, bags), 0) < lax.broadcasted_iota(i32, (bags, bags), 1)
    earlier = jnp.where(earlier, 1.0, 0.0).astype(bf16)
    lane = lax.broadcasted_iota(i32, (count * cap, bags), 0)
    packed = jnp.zeros((2 * here, count * cap), f32)
    some = 4
    line = lax.broadcasted_iota(i32, (some * cap, bags), 0)
    for q in range(count):
        lg = near_ref[q, :, :depth]
        for f in range(features):
            block = lax.dot_general(lg, w_ref[f * width : (f + 1) * width, :], NT, preferred_element_type=f32)
            g_ref[f * samples : (f + 1) * samples, :] = block.astype(bf16)
        keys = jnp.transpose(near_ref[q, :, depth:].astype(f32))

        def pick(kind, j):
            at = [kind * KEYS + f * per_bag + j for f in range(features)]
            return jnp.concatenate([keys[i : i + 1, :] for i in at], axis=1)

        owners = [pick(0, j).astype(i32) - first_ref[0] for j in range(per_bag)]
        members = [jnp.where(own == group, 1.0, 0.0) for own in owners]
        stacked = jnp.concatenate(members, axis=0).astype(bf16)
        prefix = jnp.dot(stacked, earlier, preferred_element_type=f32)
        base = jnp.zeros((here, 1), f32)
        for j in range(per_bag):
            member = members[j]
            pos = jnp.sum(member * (prefix[j * here : (j + 1) * here] + base), axis=0, keepdims=True).astype(i32)
            base = base + jnp.sum(member, axis=1, keepdims=True)
            aim_ref[j : j + 1, :] = owners[j] * cap + pos
            place = jnp.where(pos + q * cap == lane, 1.0, 0.0).astype(bf16)
            parts = jnp.concatenate([member * pick(1, j), member * pick(2, j)], axis=0).astype(bf16)
            packed = packed + lax.dot_general(parts, place, NT, preferred_element_type=f32)

        def step(i, carry):
            start = i * some * cap
            aim = aim_ref[:per_bag, :] - start
            hit = aim[0:1, :] == line
            for j in range(1, per_bag):
                hit = hit | (aim[j : j + 1, :] == line)
            chosen = jnp.where(hit, 1.0, 0.0).astype(bf16)
            out = jnp.dot(chosen, g_ref[...], preferred_element_type=f32).astype(bf16)
            for k in range(some):
                out_ref[i * some + k, q * cap : (q + 1) * cap, :] = out[k * cap : (k + 1) * cap]
            return carry

        for i in range(here // some):
            step(i, 0)
    slots_ref[...] = packed
    row = lax.broadcasted_iota(i32, (EXTRA, width), 0)
    for d in range(here):
        extra = jnp.where(row == 0, slots_ref[d : d + 1, :], 0.0)
        extra = jnp.where(row == 1, slots_ref[here + d : here + d + 1, :], extra)
        out_ref[d, count * cap :, :] = extra.astype(bf16)


def vmem():
    return pl.BlockSpec(memory_space=pltpu.VMEM)


def limit():
    return pltpu.CompilerParams(vmem_limit_bytes=40 << 20)


def with_keys(layer_grad, bag_owner, bag_slot):
    samples = layer_grad.shape[0]
    slot = bag_slot.reshape(samples, KEYS) + 1
    keys = jnp.concatenate([bag_owner.reshape(samples, KEYS), slot >> 5, slot & 31], axis=1).astype(bf16)
    return jnp.concatenate([layer_grad, jnp.pad(keys, ((0, 0), (0, 128 - 3 * KEYS)))], axis=1)


def dispatch(first, near, dense_weight, width, here, cap):
    count, samples = near.shape[0], near.shape[1]
    features = dense_weight.shape[0] // width
    return pl.pallas_call(
        lambda *refs: dispatch_kernel(here, cap, *refs),
        out_shape=jax.ShapeDtypeStruct((here, count * cap + EXTRA, width), bf16),
        in_specs=[pl.BlockSpec(memory_space=pltpu.SMEM)] + [vmem()] * 2,
        out_specs=vmem(),
        scratch_shapes=[pltpu.VMEM((samples * features, width), bf16), pltpu.VMEM((2 * here, width), f32), pltpu.VMEM((8, samples * features), i32)],
        compiler_params=limit(),
        name="dispatch",
    )(first, near, dense_weight)


def collect(got, touch):
    here, height, width = got.shape
    many = height - EXTRA
    slots = got[:, many].astype(f32) * 32.0 + got[:, many + 1].astype(f32) - 1.0
    slots = jnp.pad(slots.astype(i32), ((0, 0), (0, EXTRA)), constant_values=-1)
    selector = (jnp.arange(touch, dtype=i32)[:, None] == slots.reshape(1, -1)).astype(bf16)
    return jnp.dot(selector, got.reshape(-1, width), preferred_element_type=f32)


def update_kernel(sums_ref, old_ref, accum_ref, out_ref):
    parts, part, width = sums_ref.shape
    total = sums_ref[0]
    for k in range(1, parts):
        total = total + sums_ref[k]
    new_accum = accum_ref[...] + jnp.mean(total * total, axis=1, keepdims=True)
    updated = old_ref[...] - 0.1 * total / (jnp.sqrt(new_accum) + 1e-06)
    lowest = jnp.min(updated, axis=1, keepdims=True)
    highest = jnp.max(updated, axis=1, keepdims=True)
    new_scale = (highest - lowest) / 255.0
    new_codes = (updated - lowest) / new_scale
    diagonal = lax.broadcasted_iota(i32, (part, part), 0) == lax.broadcasted_iota(i32, (part, part), 1)
    row = lax.broadcasted_iota(i32, (8, part), 0)
    small = jnp.zeros((8, part), f32)
    for i, column in enumerate((new_scale, lowest, new_accum)):
        flat = jnp.sum(jnp.where(diagonal, column, 0.0), axis=0, keepdims=True)
        small = jnp.where(row == i, flat, small)
    small = jnp.concatenate([small, jnp.zeros((8, width - part), f32)], axis=1)
    for k in range(parts):
        out_ref[k, :part, :] = new_codes
        out_ref[k, part:, :] = small


def update(sums, old, old_accum):
    parts, part, width = sums.shape
    return pl.pallas_call(
        update_kernel,
        out_shape=jax.ShapeDtypeStruct((parts, part + 8, width), f32),
        in_specs=[vmem()] * 3,
        out_specs=vmem(),
        compiler_params=limit(),
        name="update",
    )(sums, old, old_accum[:, None])


def swap(a, axis, size, bit):
    return lax.ppermute(a, axis, [(i, i ^ bit) for i in range(size)])


def halve(a, axis, size, bit, dim):
    side = (lax.axis_index(axis) & bit) // bit
    n = a.shape[dim] // 2
    keep = lax.dynamic_slice_in_dim(a, side * n, n, dim)
    send = lax.dynamic_slice_in_dim(a, (1 - side) * n, n, dim)
    return keep + swap(send, axis, size, bit)


def double(a, axis, size, bit, dim):
    other = swap(a, axis, size, bit)
    first = (lax.axis_index(axis) & bit) == 0
    return jnp.concatenate([jnp.where(first, a, other), jnp.where(first, other, a)], axis=dim)


def shift(a, axis, size, k):
    return lax.ppermute(a, axis, [(i, (i + k) % size) for i in range(size)])


def tie(*arrays):
    return lax.optimization_barrier(arrays)


def sum_over_three(a):
    me = lax.axis_index("zl")
    got = [a] + [shift(a, "zl", NZL, k) for k in range(1, NZL)]
    total = None
    for source in range(NZL):
        term = got[NZL - 1]
        for k in range(NZL - 1):
            term = jnp.where((me - k) % NZL == source, got[k], term)
        total = term if total is None else total + term
    return total


def shards(pooled, layer_grad, dense_weight, bag_owner, bag_slot, touched, codes, row_scale, row_bias, accum):
    here = NY * NC
    parts = NX * NZL
    width = codes.shape[1]
    touch = touched.shape[0]
    part = touch // parts
    cap = 2 * bag_slot.shape[0] // (NZH * here)
    first = (lax.axis_index("zh") * here).astype(i32).reshape(1)
    near = with_keys(layer_grad, bag_owner, bag_slot)
    near = lax.all_gather(near, "zh", axis=0, tiled=False)
    rows = dispatch(first, near, dense_weight, width, here, cap)
    rows, pooled = tie(rows, pooled)
    got = lax.all_to_all(rows, ("y", "c"), 0, 0, tiled=True)
    w = lax.dot_general(pooled, layer_grad, (((0,), (0,)), ((), ())), preferred_element_type=f32)
    w = halve(w, "c", NC, 1, 0)
    w = halve(w, "x", NX, 1, 0)
    w = halve(w, "x", NX, 2, 0)
    w = halve(w, "zh", NZH, 1, 0)
    w = halve(w, "zh", NZH, 2, 0)
    w = sum_over_three(w)
    mine = lax.axis_index("x") * NZL + lax.axis_index("zl")
    local = lax.dynamic_slice_in_dim(touched, mine * part, part, 0)
    old = codes[local].astype(f32) * row_scale[local][:, None] + row_bias[local][:, None]
    old_accum = accum[local]
    got, w, old, old_accum = tie(got, w, old, old_accum)

    sums = collect(got, touch).reshape(parts, part, width)
    sums = lax.all_to_all(sums, REP, 0, 0, tiled=True)
    for bit in (1, 2, 4):
        w = w + swap(w, "y", NY, bit)
    w = double(w, "zh", NZH, 2, 0)
    sums, w = tie(sums, w)

    payload = lax.all_to_all(update(sums, old, old_accum), REP, 0, 0, tiled=True)
    w = double(w, "zh", NZH, 1, 0)
    w = double(w, "x", NX, 2, 0)
    w = double(w, "x", NX, 1, 0)
    weight_grad = double(w, "c", NC, 1, 0)
    new_codes = payload[:, :part].reshape(touch, width)
    new_scale, lowest, new_accum = (payload[:, part + i, :part].reshape(touch) for i in range(3))
    return (weight_grad, new_codes, new_scale, lowest, new_accum)


def solution(mesh):
    mesh = Mesh(mesh.devices.reshape(NX, NZL, NZH, NY, NC), AXES)
    in_specs = (
        P(AXES, None),
        P(AXES, None),
        P(),
        P(AXES, None),
        P(AXES),
        P(SHARD),
        P(SHARD, None),
        P(SHARD),
        P(SHARD),
        P(SHARD),
    )
    out_specs = (P(), P(SHARD, None), P(SHARD), P(SHARD), P(SHARD))
    return jax.shard_map(shards, mesh=mesh, in_specs=in_specs, out_specs=out_specs, check_vma=False)
```

```python
import jax
import jax.numpy as jnp
from jax import lax
from jax.experimental import pallas as pl
from jax.experimental.pallas import tpu as pltpu
from jax.sharding import Mesh, PartitionSpec as P

f32, bf16, i32 = jnp.float32, jnp.bfloat16, jnp.int32
NX, NZL, NZH, NY, NC = 4, 3, 4, 8, 2
AXES = ("x", "zl", "zh", "y", "c")
REP = ("x", "zl")
SHARD = ("zh", "y", "c")
KEYS, EXTRA = 16, 16
NT = (((1,), (1,)), ((), ()))


def dispatch_kernel(here, cap, first_ref, near_ref, w_ref, out_ref, g_ref, slots_ref, aim_ref):
    count, samples = near_ref.shape[0], near_ref.shape[1]
    depth = w_ref.shape[1]
    width = out_ref.shape[2]
    features = w_ref.shape[0] // width
    bags = samples * features
    per_bag = KEYS // features
    group = lax.broadcasted_iota(i32, (here, bags), 0)
    earlier = lax.broadcasted_iota(i32, (bags, bags), 0) < lax.broadcasted_iota(i32, (bags, bags), 1)
    earlier = jnp.where(earlier, 1.0, 0.0).astype(bf16)
    lane = lax.broadcasted_iota(i32, (count * cap, bags), 0)
    packed = jnp.zeros((2 * here, count * cap), f32)
    some = 4
    line = lax.broadcasted_iota(i32, (some * cap, bags), 0)
    for q in range(count):
        lg = near_ref[q, :, :depth]
        for f in range(features):
            block = lax.dot_general(lg, w_ref[f * width : (f + 1) * width, :], NT, preferred_element_type=f32)
            g_ref[f * samples : (f + 1) * samples, :] = block.astype(bf16)
        keys = jnp.transpose(near_ref[q, :, depth:].astype(f32))

        def pick(kind, j):
            at = [kind * KEYS + f * per_bag + j for f in range(features)]
            return jnp.concatenate([keys[i : i + 1, :] for i in at], axis=1)

        owners = [pick(0, j).astype(i32) - first_ref[0] for j in range(per_bag)]
        members = [jnp.where(own == group, 1.0, 0.0) for own in owners]
        stacked = jnp.concatenate(members, axis=0).astype(bf16)
        prefix = jnp.dot(stacked, earlier, preferred_element_type=f32)
        base = jnp.zeros((here, 1), f32)
        for j in range(per_bag):
            member = members[j]
            pos = jnp.sum(member * (prefix[j * here : (j + 1) * here] + base), axis=0, keepdims=True).astype(i32)
            base = base + jnp.sum(member, axis=1, keepdims=True)
            aim_ref[j : j + 1, :] = owners[j] * cap + pos
            place = jnp.where(pos + q * cap == lane, 1.0, 0.0).astype(bf16)
            parts = jnp.concatenate([member * pick(1, j), member * pick(2, j)], axis=0).astype(bf16)
            packed = packed + lax.dot_general(parts, place, NT, preferred_element_type=f32)

        def step(i, carry):
            start = i * some * cap
            aim = aim_ref[:per_bag, :] - start
            hit = aim[0:1, :] == line
            for j in range(1, per_bag):
                hit = hit | (aim[j : j + 1, :] == line)
            chosen = jnp.where(hit, 1.0, 0.0).astype(bf16)
            out = jnp.dot(chosen, g_ref[...], preferred_element_type=f32).astype(bf16)
            for k in range(some):
                out_ref[i * some + k, q * cap : (q + 1) * cap, :] = out[k * cap : (k + 1) * cap]
            return carry

        for i in range(here // some):
            step(i, 0)
    slots_ref[...] = packed
    row = lax.broadcasted_iota(i32, (EXTRA, width), 0)
    for d in range(here):
        extra = jnp.where(row == 0, slots_ref[d : d + 1, :], 0.0)
        extra = jnp.where(row == 1, slots_ref[here + d : here + d + 1, :], extra)
        out_ref[d, count * cap :, :] = extra.astype(bf16)


def vmem():
    return pl.BlockSpec(memory_space=pltpu.VMEM)


def limit():
    return pltpu.CompilerParams(vmem_limit_bytes=40 << 20)


def with_keys(layer_grad, bag_owner, bag_slot):
    samples = layer_grad.shape[0]
    slot = bag_slot.reshape(samples, KEYS) + 1
    keys = jnp.concatenate([bag_owner.reshape(samples, KEYS), slot >> 5, slot & 31], axis=1).astype(bf16)
    return jnp.concatenate([layer_grad, jnp.pad(keys, ((0, 0), (0, 128 - 3 * KEYS)))], axis=1)


def dispatch(first, near, dense_weight, width, here, cap):
    count, samples = near.shape[0], near.shape[1]
    features = dense_weight.shape[0] // width
    return pl.pallas_call(
        lambda *refs: dispatch_kernel(here, cap, *refs),
        out_shape=jax.ShapeDtypeStruct((here, count * cap + EXTRA, width), bf16),
        in_specs=[pl.BlockSpec(memory_space=pltpu.SMEM)] + [vmem()] * 2,
        out_specs=vmem(),
        scratch_shapes=[pltpu.VMEM((samples * features, width), bf16), pltpu.VMEM((2 * here, width), f32), pltpu.VMEM((8, samples * features), i32)],
        compiler_params=limit(),
        name="dispatch",
    )(first, near, dense_weight)


def collect(got, touch):
    here, height, width = got.shape
    many = height - EXTRA
    slots = got[:, many].astype(f32) * 32.0 + got[:, many + 1].astype(f32) - 1.0
    slots = jnp.pad(slots.astype(i32), ((0, 0), (0, EXTRA)), constant_values=-1)
    selector = (jnp.arange(touch, dtype=i32)[:, None] == slots.reshape(1, -1)).astype(bf16)
    return jnp.dot(selector, got.reshape(-1, width), preferred_element_type=f32)


def update_kernel(sums_ref, old_ref, accum_ref, out_ref):
    parts, part, width = sums_ref.shape
    total = sums_ref[0]
    for k in range(1, parts):
        total = total + sums_ref[k]
    new_accum = accum_ref[...] + jnp.mean(total * total, axis=1, keepdims=True)
    updated = old_ref[...] - 0.1 * total / (jnp.sqrt(new_accum) + 1e-06)
    lowest = jnp.min(updated, axis=1, keepdims=True)
    highest = jnp.max(updated, axis=1, keepdims=True)
    new_scale = (highest - lowest) / 255.0
    new_codes = (updated - lowest) / new_scale
    diagonal = lax.broadcasted_iota(i32, (part, part), 0) == lax.broadcasted_iota(i32, (part, part), 1)
    row = lax.broadcasted_iota(i32, (8, part), 0)
    small = jnp.zeros((8, part), f32)
    for i, column in enumerate((new_scale, lowest, new_accum)):
        flat = jnp.sum(jnp.where(diagonal, column, 0.0), axis=0, keepdims=True)
        small = jnp.where(row == i, flat, small)
    small = jnp.concatenate([small, jnp.zeros((8, width - part), f32)], axis=1)
    for k in range(parts):
        out_ref[k, :part, :] = new_codes
        out_ref[k, part:, :] = small


def update(sums, old, old_accum):
    parts, part, width = sums.shape
    return pl.pallas_call(
        update_kernel,
        out_shape=jax.ShapeDtypeStruct((parts, part + 8, width), f32),
        in_specs=[vmem()] * 3,
        out_specs=vmem(),
        compiler_params=limit(),
        name="update",
    )(sums, old, old_accum[:, None])


def swap(a, axis, size, bit):
    return lax.ppermute(a, axis, [(i, i ^ bit) for i in range(size)])


def halve(a, axis, size, bit, dim):
    side = (lax.axis_index(axis) & bit) // bit
    n = a.shape[dim] // 2
    keep = lax.dynamic_slice_in_dim(a, side * n, n, dim)
    send = lax.dynamic_slice_in_dim(a, (1 - side) * n, n, dim)
    return keep + swap(send, axis, size, bit)


def scatter_sum(a, axis, size):
    me = lax.axis_index(axis)
    n = a.shape[0] // size

    def block(k):
        return lax.dynamic_slice_in_dim(a, lax.rem(me + k, size) * n, n, 0)

    got = [shift(block(k), axis, size, k) for k in range(1, size)]
    total = block(0)
    for g in got:
        total = total + g
    return total


def gather(a, axis, size):
    me = lax.axis_index(axis)
    n = a.shape[0]
    got = [shift(a, axis, size, k) for k in range(1, size)]
    out = jnp.concatenate([a] * size, axis=0)
    for k, piece in enumerate(got, 1):
        out = lax.dynamic_update_slice_in_dim(out, piece, lax.rem(me - k + size, size) * n, 0)
    return out


def shift(a, axis, size, k):
    return lax.ppermute(a, axis, [(i, (i + k) % size) for i in range(size)])


def tie(*arrays):
    return lax.optimization_barrier(arrays)


def sum_over_three(a):
    me = lax.axis_index("zl")
    got = [a] + [shift(a, "zl", NZL, k) for k in range(1, NZL)]
    total = None
    for source in range(NZL):
        term = got[NZL - 1]
        for k in range(NZL - 1):
            term = jnp.where((me - k) % NZL == source, got[k], term)
        total = term if total is None else total + term
    return total


def shards(pooled, layer_grad, dense_weight, bag_owner, bag_slot, touched, codes, row_scale, row_bias, accum):
    here = NY * NC
    parts = NX * NZL
    width = codes.shape[1]
    touch = touched.shape[0]
    part = touch // parts
    cap = 2 * bag_slot.shape[0] // (NZH * here)
    first = (lax.axis_index("zh") * here).astype(i32).reshape(1)
    near = with_keys(layer_grad, bag_owner, bag_slot)
    near = lax.all_gather(near, "zh", axis=0, tiled=False)
    rows = dispatch(first, near, dense_weight, width, here, cap)
    rows, pooled = tie(rows, pooled)
    got = lax.all_to_all(rows, ("y", "c"), 0, 0, tiled=True)
    w = lax.dot_general(pooled, layer_grad, (((0,), (0,)), ((), ())), preferred_element_type=f32)
    w = halve(w, "c", NC, 1, 0)
    w = scatter_sum(w, "x", NX)
    w = scatter_sum(w, "zh", NZH)
    w = sum_over_three(w)
    mine = lax.axis_index("x") * NZL + lax.axis_index("zl")
    local = lax.dynamic_slice_in_dim(touched, mine * part, part, 0)
    old = codes[local].astype(f32) * row_scale[local][:, None] + row_bias[local][:, None]
    old_accum = accum[local]
    got, w, old, old_accum = tie(got, w, old, old_accum)

    sums = collect(got, touch).reshape(parts, part, width)
    sums = lax.all_to_all(sums, REP, 0, 0, tiled=True)
    for bit in (1, 2, 4):
        w = w + swap(w, "y", NY, bit)
    sums, w = tie(sums, w)

    payload = lax.all_to_all(update(sums, old, old_accum), REP, 0, 0, tiled=True)
    w = gather(w, "zh", NZH)
    w = gather(w, "x", NX)
    weight_grad = gather(w, "c", NC)
    new_codes = payload[:, :part].reshape(touch, width)
    new_scale, lowest, new_accum = (payload[:, part + i, :part].reshape(touch) for i in range(3))
    return (weight_grad, new_codes, new_scale, lowest, new_accum)


def solution(mesh):
    mesh = Mesh(mesh.devices.reshape(NX, NZL, NZH, NY, NC), AXES)
    in_specs = (
        P(AXES, None),
        P(AXES, None),
        P(),
        P(AXES, None),
        P(AXES),
        P(SHARD),
        P(SHARD, None),
        P(SHARD),
        P(SHARD),
        P(SHARD),
    )
    out_specs = (P(), P(SHARD, None), P(SHARD), P(SHARD), P(SHARD))
    return jax.shard_map(shards, mesh=mesh, in_specs=in_specs, out_specs=out_specs, check_vma=False)
```

```python
import jax
import jax.numpy as jnp
from jax import lax
from jax.experimental import pallas as pl
from jax.experimental.pallas import tpu as pltpu
from jax.sharding import Mesh, PartitionSpec as P

f32, bf16, i32 = jnp.float32, jnp.bfloat16, jnp.int32
NX, NZL, NZH, NY, NC = 4, 3, 4, 8, 2
AXES = ("x", "zl", "zh", "y", "c")
REP = ("x", "zl")
SHARD = ("zh", "y", "c")
KEYS, EXTRA = 16, 16
NT = (((1,), (1,)), ((), ()))


def dispatch_kernel(here, cap, first_ref, near_ref, w_ref, out_ref, g_ref, slots_ref, aim_ref):
    count, samples = near_ref.shape[0], near_ref.shape[1]
    depth = w_ref.shape[1]
    width = out_ref.shape[2]
    features = w_ref.shape[0] // width
    bags = samples * features
    per_bag = KEYS // features
    group = lax.broadcasted_iota(i32, (here, bags), 0)
    earlier = lax.broadcasted_iota(i32, (bags, bags), 0) < lax.broadcasted_iota(i32, (bags, bags), 1)
    earlier = jnp.where(earlier, 1.0, 0.0).astype(bf16)
    lane = lax.broadcasted_iota(i32, (count * cap, bags), 0)
    packed = jnp.zeros((2 * here, count * cap), f32)
    some = 4
    line = lax.broadcasted_iota(i32, (some * cap, bags), 0)
    for q in range(count):
        lg = near_ref[q, :, :depth]
        for f in range(features):
            block = lax.dot_general(lg, w_ref[f * width : (f + 1) * width, :], NT, preferred_element_type=f32)
            g_ref[f * samples : (f + 1) * samples, :] = block.astype(bf16)
        keys = jnp.transpose(near_ref[q, :, depth:].astype(f32))

        def pick(kind, j):
            at = [kind * KEYS + f * per_bag + j for f in range(features)]
            return jnp.concatenate([keys[i : i + 1, :] for i in at], axis=1)

        owners = [pick(0, j).astype(i32) - first_ref[0] for j in range(per_bag)]
        members = [jnp.where(own == group, 1.0, 0.0) for own in owners]
        stacked = jnp.concatenate(members, axis=0).astype(bf16)
        prefix = jnp.dot(stacked, earlier, preferred_element_type=f32)
        base = jnp.zeros((here, 1), f32)
        for j in range(per_bag):
            member = members[j]
            pos = jnp.sum(member * (prefix[j * here : (j + 1) * here] + base), axis=0, keepdims=True).astype(i32)
            base = base + jnp.sum(member, axis=1, keepdims=True)
            aim_ref[j : j + 1, :] = owners[j] * cap + pos
            place = jnp.where(pos + q * cap == lane, 1.0, 0.0).astype(bf16)
            parts = jnp.concatenate([member * pick(1, j), member * pick(2, j)], axis=0).astype(bf16)
            packed = packed + lax.dot_general(parts, place, NT, preferred_element_type=f32)

        def step(i, carry):
            start = i * some * cap
            aim = aim_ref[:per_bag, :] - start
            hit = aim[0:1, :] == line
            for j in range(1, per_bag):
                hit = hit | (aim[j : j + 1, :] == line)
            chosen = jnp.where(hit, 1.0, 0.0).astype(bf16)
            out = jnp.dot(chosen, g_ref[...], preferred_element_type=f32).astype(bf16)
            for k in range(some):
                out_ref[i * some + k, q * cap : (q + 1) * cap, :] = out[k * cap : (k + 1) * cap]
            return carry

        for i in range(here // some):
            step(i, 0)
    slots_ref[...] = packed
    row = lax.broadcasted_iota(i32, (EXTRA, width), 0)
    for d in range(here):
        extra = jnp.where(row == 0, slots_ref[d : d + 1, :], 0.0)
        extra = jnp.where(row == 1, slots_ref[here + d : here + d + 1, :], extra)
        out_ref[d, count * cap :, :] = extra.astype(bf16)


def vmem():
    return pl.BlockSpec(memory_space=pltpu.VMEM)


def limit():
    return pltpu.CompilerParams(vmem_limit_bytes=40 << 20)


def with_keys(layer_grad, bag_owner, bag_slot):
    samples = layer_grad.shape[0]
    slot = bag_slot.reshape(samples, KEYS) + 1
    keys = jnp.concatenate([bag_owner.reshape(samples, KEYS), slot >> 5, slot & 31], axis=1).astype(bf16)
    return jnp.concatenate([layer_grad, jnp.pad(keys, ((0, 0), (0, 128 - 3 * KEYS)))], axis=1)


def dispatch(first, near, dense_weight, width, here, cap):
    count, samples = near.shape[0], near.shape[1]
    features = dense_weight.shape[0] // width
    return pl.pallas_call(
        lambda *refs: dispatch_kernel(here, cap, *refs),
        out_shape=jax.ShapeDtypeStruct((here, count * cap + EXTRA, width), bf16),
        in_specs=[pl.BlockSpec(memory_space=pltpu.SMEM)] + [vmem()] * 2,
        out_specs=vmem(),
        scratch_shapes=[pltpu.VMEM((samples * features, width), bf16), pltpu.VMEM((2 * here, width), f32), pltpu.VMEM((8, samples * features), i32)],
        compiler_params=limit(),
        name="dispatch",
    )(first, near, dense_weight)


def collect(got, touch):
    here, height, width = got.shape
    many = height - EXTRA
    slots = got[:, many].astype(f32) * 32.0 + got[:, many + 1].astype(f32) - 1.0
    slots = jnp.pad(slots.astype(i32), ((0, 0), (0, EXTRA)), constant_values=-1)
    selector = (jnp.arange(touch, dtype=i32)[:, None] == slots.reshape(1, -1)).astype(bf16)
    return jnp.dot(selector, got.reshape(-1, width), preferred_element_type=f32)


def update_kernel(sums_ref, old_ref, accum_ref, out_ref):
    parts, part, width = sums_ref.shape
    total = sums_ref[0]
    for k in range(1, parts):
        total = total + sums_ref[k]
    new_accum = accum_ref[...] + jnp.mean(total * total, axis=1, keepdims=True)
    updated = old_ref[...] - 0.1 * total / (jnp.sqrt(new_accum) + 1e-06)
    lowest = jnp.min(updated, axis=1, keepdims=True)
    highest = jnp.max(updated, axis=1, keepdims=True)
    new_scale = (highest - lowest) / 255.0
    new_codes = (updated - lowest) / new_scale
    diagonal = lax.broadcasted_iota(i32, (part, part), 0) == lax.broadcasted_iota(i32, (part, part), 1)
    row = lax.broadcasted_iota(i32, (8, part), 0)
    small = jnp.zeros((8, part), f32)
    for i, column in enumerate((new_scale, lowest, new_accum)):
        flat = jnp.sum(jnp.where(diagonal, column, 0.0), axis=0, keepdims=True)
        small = jnp.where(row == i, flat, small)
    small = jnp.concatenate([small, jnp.zeros((8, width - part), f32)], axis=1)
    for k in range(parts):
        out_ref[k, :part, :] = new_codes
        out_ref[k, part:, :] = small


def update(sums, old, old_accum):
    parts, part, width = sums.shape
    return pl.pallas_call(
        update_kernel,
        out_shape=jax.ShapeDtypeStruct((parts, part + 8, width), f32),
        in_specs=[vmem()] * 3,
        out_specs=vmem(),
        compiler_params=limit(),
        name="update",
    )(sums, old, old_accum[:, None])


def swap(a, axis, size, bit):
    return lax.ppermute(a, axis, [(i, i ^ bit) for i in range(size)])


def halve(a, axis, size, bit, dim):
    side = (lax.axis_index(axis) & bit) // bit
    n = a.shape[dim] // 2
    keep = lax.dynamic_slice_in_dim(a, side * n, n, dim)
    send = lax.dynamic_slice_in_dim(a, (1 - side) * n, n, dim)
    return keep + swap(send, axis, size, bit)


def scatter_sum(a, axis, size):
    me = lax.axis_index(axis)
    n = a.shape[0] // size

    def block(k):
        return lax.dynamic_slice_in_dim(a, lax.rem(me + k, size) * n, n, 0)

    got = [shift(block(k), axis, size, k) for k in range(1, size)]
    total = block(0)
    for g in got:
        total = total + g
    return total


def gather(a, axis, size, dim=0):
    me = lax.axis_index(axis)
    n = a.shape[dim]
    got = [shift(a, axis, size, k) for k in range(1, size)]
    out = jnp.concatenate([a] * size, axis=dim)
    for k, piece in enumerate(got, 1):
        out = lax.dynamic_update_slice_in_dim(out, piece, lax.rem(me - k + size, size) * n, dim)
    return out


def shift(a, axis, size, k):
    return lax.ppermute(a, axis, [(i, (i + k) % size) for i in range(size)])


def tie(*arrays):
    return lax.optimization_barrier(arrays)


def double(a, axis, size, bit, dim):
    other = swap(a, axis, size, bit)
    first = (lax.axis_index(axis) & bit) == 0
    return jnp.concatenate([jnp.where(first, a, other), jnp.where(first, other, a)], axis=dim)


def exchange_columns(a, axis, size):
    me = lax.axis_index(axis)
    n = a.shape[1] // size

    def block(k):
        return lax.dynamic_slice_in_dim(a, lax.rem(me + k, size) * n, n, 1)

    got = [shift(block(k), axis, size, k) for k in range(1, size)]
    return [block(0)] + got


def sum_over_three(a):
    me = lax.axis_index("zl")
    got = [a] + [shift(a, "zl", NZL, k) for k in range(1, NZL)]
    total = None
    for source in range(NZL):
        term = got[NZL - 1]
        for k in range(NZL - 1):
            term = jnp.where((me - k) % NZL == source, got[k], term)
        total = term if total is None else total + term
    return total


def shards(pooled, layer_grad, dense_weight, bag_owner, bag_slot, touched, codes, row_scale, row_bias, accum):
    here = NY * NC
    parts = NX * NZL
    width = codes.shape[1]
    touch = touched.shape[0]
    part = touch // parts
    cap = 2 * bag_slot.shape[0] // (NZH * here)
    first = (lax.axis_index("zh") * here).astype(i32).reshape(1)
    near = with_keys(layer_grad, bag_owner, bag_slot)
    columns = exchange_columns(pooled, "zh", NZH)
    near = lax.all_gather(near, "zh", axis=0, tiled=False)
    near, *columns = tie(near, *columns)
    rows = dispatch(first, near, dense_weight, width, here, cap)
    rows, near, *columns = tie(rows, near, *columns)
    got = lax.all_to_all(rows, ("y", "c"), 0, 0, tiled=True)
    level = lax.axis_index("zh")
    lower = [lax.rem(level - k + NZH, NZH) for k in range(NZH)]
    lg = [lax.dynamic_index_in_dim(near, at, 0, keepdims=False)[:, : layer_grad.shape[1]] for at in lower]
    w = lax.dot_general(jnp.concatenate(columns, axis=0), jnp.concatenate(lg, axis=0), (((0,), (0,)), ((), ())), preferred_element_type=f32)
    w = halve(w, "c", NC, 1, 0)
    w = scatter_sum(w, "x", NX)
    w = gather(sum_over_three(w)[None], "zh", NZH)
    mine = lax.axis_index("x") * NZL + lax.axis_index("zl")
    local = lax.dynamic_slice_in_dim(touched, mine * part, part, 0)
    old = codes[local].astype(f32) * row_scale[local][:, None] + row_bias[local][:, None]
    old_accum = accum[local]
    got, w, old, old_accum = tie(got, w, old, old_accum)

    sums = collect(got, touch).reshape(parts, part, width)
    sums = lax.all_to_all(sums, REP, 0, 0, tiled=True)
    w = halve(w, "y", NY, 1, 0)
    w = halve(w, "y", NY, 2, 0)
    w = w + swap(w, "y", NY, 4)
    sums, w = tie(sums, w)

    payload = lax.all_to_all(update(sums, old, old_accum), REP, 0, 0, tiled=True)
    w = double(w, "y", NY, 2, 0)
    w = double(w, "y", NY, 1, 0)
    w = gather(w, "x", NX, 1)
    new_codes = payload[:, :part].reshape(touch, width)
    new_scale, lowest, new_accum = (payload[:, part + i, :part].reshape(touch) for i in range(3))
    w, new_codes, new_scale, lowest, new_accum = tie(w, new_codes, new_scale, lowest, new_accum)
    weight_grad = gather(w, "c", NC, 1).reshape(pooled.shape[1], layer_grad.shape[1])
    return (weight_grad, new_codes, new_scale, lowest, new_accum)


def solution(mesh):
    mesh = Mesh(mesh.devices.reshape(NX, NZL, NZH, NY, NC), AXES)
    in_specs = (
        P(AXES, None),
        P(AXES, None),
        P(),
        P(AXES, None),
        P(AXES),
        P(SHARD),
        P(SHARD, None),
        P(SHARD),
        P(SHARD),
        P(SHARD),
    )
    out_specs = (P(), P(SHARD, None), P(SHARD), P(SHARD), P(SHARD))
    return jax.shard_map(shards, mesh=mesh, in_specs=in_specs, out_specs=out_specs, check_vma=False)
```

```python
import jax
import jax.numpy as jnp
from jax import lax
from jax.experimental import pallas as pl
from jax.experimental.pallas import tpu as pltpu
from jax.sharding import Mesh, PartitionSpec as P

f32, bf16, i32 = jnp.float32, jnp.bfloat16, jnp.int32
NX, NZL, NZH, NY, NC = 4, 3, 4, 8, 2
AXES = ("x", "zl", "zh", "y", "c")
REP = ("x", "zl")
SHARD = ("zh", "y", "c")
KEYS, EXTRA = 16, 16
NT = (((1,), (1,)), ((), ()))


def dispatch_kernel(here, cap, first_ref, near_ref, w_ref, out_ref, g_ref, slots_ref, aim_ref):
    count, samples = near_ref.shape[0], near_ref.shape[1]
    depth = w_ref.shape[1]
    width = out_ref.shape[2]
    features = w_ref.shape[0] // width
    bags = samples * features
    per_bag = KEYS // features
    group = lax.broadcasted_iota(i32, (here, bags), 0)
    earlier = lax.broadcasted_iota(i32, (bags, bags), 0) < lax.broadcasted_iota(i32, (bags, bags), 1)
    earlier = jnp.where(earlier, 1.0, 0.0).astype(bf16)
    lane = lax.broadcasted_iota(i32, (count * cap, bags), 0)
    packed = jnp.zeros((2 * here, count * cap), f32)
    some = 4
    line = lax.broadcasted_iota(i32, (some * cap, bags), 0)
    for q in range(count):
        lg = near_ref[q, :, :depth]
        for f in range(features):
            block = lax.dot_general(lg, w_ref[f * width : (f + 1) * width, :], NT, preferred_element_type=f32)
            g_ref[f * samples : (f + 1) * samples, :] = block.astype(bf16)
        keys = jnp.transpose(near_ref[q, :, depth:].astype(f32))

        def pick(kind, j):
            at = [kind * KEYS + f * per_bag + j for f in range(features)]
            return jnp.concatenate([keys[i : i + 1, :] for i in at], axis=1)

        owners = [pick(0, j).astype(i32) - first_ref[0] for j in range(per_bag)]
        members = [jnp.where(own == group, 1.0, 0.0) for own in owners]
        stacked = jnp.concatenate(members, axis=0).astype(bf16)
        prefix = jnp.dot(stacked, earlier, preferred_element_type=f32)
        base = jnp.zeros((here, 1), f32)
        for j in range(per_bag):
            member = members[j]
            pos = jnp.sum(member * (prefix[j * here : (j + 1) * here] + base), axis=0, keepdims=True).astype(i32)
            base = base + jnp.sum(member, axis=1, keepdims=True)
            aim_ref[j : j + 1, :] = owners[j] * cap + pos
            place = jnp.where(pos + q * cap == lane, 1.0, 0.0).astype(bf16)
            parts = jnp.concatenate([member * pick(1, j), member * pick(2, j)], axis=0).astype(bf16)
            packed = packed + lax.dot_general(parts, place, NT, preferred_element_type=f32)

        def step(i, carry):
            start = i * some * cap
            aim = aim_ref[:per_bag, :] - start
            hit = aim[0:1, :] == line
            for j in range(1, per_bag):
                hit = hit | (aim[j : j + 1, :] == line)
            chosen = jnp.where(hit, 1.0, 0.0).astype(bf16)
            out = jnp.dot(chosen, g_ref[...], preferred_element_type=f32).astype(bf16)
            for k in range(some):
                out_ref[i * some + k, q * cap : (q + 1) * cap, :] = out[k * cap : (k + 1) * cap]
            return carry

        for i in range(here // some):
            step(i, 0)
    slots_ref[...] = packed
    row = lax.broadcasted_iota(i32, (EXTRA, width), 0)
    for d in range(here):
        extra = jnp.where(row == 0, slots_ref[d : d + 1, :], 0.0)
        extra = jnp.where(row == 1, slots_ref[here + d : here + d + 1, :], extra)
        out_ref[d, count * cap :, :] = extra.astype(bf16)


def vmem():
    return pl.BlockSpec(memory_space=pltpu.VMEM)


def limit():
    return pltpu.CompilerParams(vmem_limit_bytes=40 << 20)


def with_keys(layer_grad, bag_owner, bag_slot):
    samples = layer_grad.shape[0]
    slot = bag_slot.reshape(samples, KEYS) + 1
    keys = jnp.concatenate([bag_owner.reshape(samples, KEYS), slot >> 5, slot & 31], axis=1).astype(bf16)
    return jnp.concatenate([layer_grad, jnp.pad(keys, ((0, 0), (0, 128 - 3 * KEYS)))], axis=1)


def dispatch(first, near, dense_weight, width, here, cap):
    count, samples = near.shape[0], near.shape[1]
    features = dense_weight.shape[0] // width
    return pl.pallas_call(
        lambda *refs: dispatch_kernel(here, cap, *refs),
        out_shape=jax.ShapeDtypeStruct((here, count * cap + EXTRA, width), bf16),
        in_specs=[pl.BlockSpec(memory_space=pltpu.SMEM)] + [vmem()] * 2,
        out_specs=vmem(),
        scratch_shapes=[pltpu.VMEM((samples * features, width), bf16), pltpu.VMEM((2 * here, width), f32), pltpu.VMEM((8, samples * features), i32)],
        compiler_params=limit(),
        name="dispatch",
    )(first, near, dense_weight)


def collect(got, touch):
    here, height, width = got.shape
    many = height - EXTRA
    slots = got[:, many].astype(f32) * 32.0 + got[:, many + 1].astype(f32) - 1.0
    slots = jnp.pad(slots.astype(i32), ((0, 0), (0, EXTRA)), constant_values=-1)
    selector = (jnp.arange(touch, dtype=i32)[:, None] == slots.reshape(1, -1)).astype(bf16)
    return jnp.dot(selector, got.reshape(-1, width), preferred_element_type=f32)


def update_kernel(sums_ref, old_ref, accum_ref, out_ref):
    parts, part, width = sums_ref.shape
    total = sums_ref[0]
    for k in range(1, parts):
        total = total + sums_ref[k]
    new_accum = accum_ref[...] + jnp.mean(total * total, axis=1, keepdims=True)
    updated = old_ref[...] - 0.1 * total / (jnp.sqrt(new_accum) + 1e-06)
    lowest = jnp.min(updated, axis=1, keepdims=True)
    highest = jnp.max(updated, axis=1, keepdims=True)
    new_scale = (highest - lowest) / 255.0
    new_codes = (updated - lowest) / new_scale
    diagonal = lax.broadcasted_iota(i32, (part, part), 0) == lax.broadcasted_iota(i32, (part, part), 1)
    row = lax.broadcasted_iota(i32, (8, part), 0)
    small = jnp.zeros((8, part), f32)
    for i, column in enumerate((new_scale, lowest, new_accum)):
        flat = jnp.sum(jnp.where(diagonal, column, 0.0), axis=0, keepdims=True)
        small = jnp.where(row == i, flat, small)
    small = jnp.concatenate([small, jnp.zeros((8, width - part), f32)], axis=1)
    for k in range(parts):
        out_ref[k, :part, :] = new_codes
        out_ref[k, part:, :] = small


def update(sums, old, old_accum):
    parts, part, width = sums.shape
    return pl.pallas_call(
        update_kernel,
        out_shape=jax.ShapeDtypeStruct((parts, part + 8, width), f32),
        in_specs=[vmem()] * 3,
        out_specs=vmem(),
        compiler_params=limit(),
        name="update",
    )(sums, old, old_accum[:, None])


def swap(a, axis, size, bit):
    return lax.ppermute(a, axis, [(i, i ^ bit) for i in range(size)])


def halve(a, axis, size, bit, dim):
    side = (lax.axis_index(axis) & bit) // bit
    n = a.shape[dim] // 2
    keep = lax.dynamic_slice_in_dim(a, side * n, n, dim)
    send = lax.dynamic_slice_in_dim(a, (1 - side) * n, n, dim)
    return keep + swap(send, axis, size, bit)


def scatter_sum(a, axis, size):
    me = lax.axis_index(axis)
    n = a.shape[0] // size

    def block(k):
        return lax.dynamic_slice_in_dim(a, lax.rem(me + k, size) * n, n, 0)

    got = [shift(block(k), axis, size, k) for k in range(1, size)]
    total = block(0)
    for g in got:
        total = total + g
    return total


def gather(a, axis, size, dim=0):
    me = lax.axis_index(axis)
    n = a.shape[dim]
    got = [shift(a, axis, size, k) for k in range(1, size)]
    out = jnp.concatenate([a] * size, axis=dim)
    for k, piece in enumerate(got, 1):
        out = lax.dynamic_update_slice_in_dim(out, piece, lax.rem(me - k + size, size) * n, dim)
    return out


def shift(a, axis, size, k):
    return lax.ppermute(a, axis, [(i, (i + k) % size) for i in range(size)])


def tie(*arrays):
    return lax.optimization_barrier(arrays)


def double(a, axis, size, bit, dim):
    other = swap(a, axis, size, bit)
    first = (lax.axis_index(axis) & bit) == 0
    return jnp.concatenate([jnp.where(first, a, other), jnp.where(first, other, a)], axis=dim)


def sum_over_three(a):
    me = lax.axis_index("zl")
    got = [a] + [shift(a, "zl", NZL, k) for k in range(1, NZL)]
    total = None
    for source in range(NZL):
        term = got[NZL - 1]
        for k in range(NZL - 1):
            term = jnp.where((me - k) % NZL == source, got[k], term)
        total = term if total is None else total + term
    return total


def shards(pooled, layer_grad, dense_weight, bag_owner, bag_slot, touched, codes, row_scale, row_bias, accum):
    here = NY * NC
    parts = NX * NZL
    width = codes.shape[1]
    touch = touched.shape[0]
    part = touch // parts
    cap = 2 * bag_slot.shape[0] // (NZH * here)
    first = (lax.axis_index("zh") * here).astype(i32).reshape(1)
    near = with_keys(layer_grad, bag_owner, bag_slot)
    columns = jnp.stack(jnp.split(pooled, NZH, axis=1))
    columns = lax.all_to_all(columns, "zh", 0, 0, tiled=True)
    near = lax.all_gather(near, "zh", axis=0, tiled=False)
    near, columns = tie(near, columns)
    rows = dispatch(first, near, dense_weight, width, here, cap)
    rows, near, columns = tie(rows, near, columns)
    got = lax.all_to_all(rows, ("y", "c"), 0, 0, tiled=True)
    lg = near.reshape(-1, near.shape[2])[:, : layer_grad.shape[1]]
    columns = columns.reshape(lg.shape[0], -1)
    w = lax.dot_general(columns, lg, (((0,), (0,)), ((), ())), preferred_element_type=f32)
    w = halve(w, "c", NC, 1, 0)
    w = scatter_sum(w, "x", NX)
    w = gather(sum_over_three(w)[None], "zh", NZH)
    mine = lax.axis_index("x") * NZL + lax.axis_index("zl")
    local = lax.dynamic_slice_in_dim(touched, mine * part, part, 0)
    old = codes[local].astype(f32) * row_scale[local][:, None] + row_bias[local][:, None]
    old_accum = accum[local]
    got, w, old, old_accum = tie(got, w, old, old_accum)

    sums = collect(got, touch).reshape(parts, part, width)
    sums = lax.all_to_all(sums, REP, 0, 0, tiled=True)
    w = halve(w, "y", NY, 1, 0)
    w = halve(w, "y", NY, 2, 0)
    w = w + swap(w, "y", NY, 4)
    sums, w = tie(sums, w)

    payload = lax.all_to_all(update(sums, old, old_accum), REP, 0, 0, tiled=True)
    w = double(w, "y", NY, 2, 0)
    w = double(w, "y", NY, 1, 0)
    w = gather(w, "x", NX, 1)
    new_codes = payload[:, :part].reshape(touch, width)
    new_scale, lowest, new_accum = (payload[:, part + i, :part].reshape(touch) for i in range(3))
    other = swap(w, "c", NC, 1)
    other, new_codes, new_scale, lowest, new_accum = tie(other, new_codes, new_scale, lowest, new_accum)
    side = lax.axis_index("c") * w.shape[1]
    weight_grad = jnp.concatenate([w, w], axis=1)
    weight_grad = lax.dynamic_update_slice_in_dim(weight_grad, other, w.shape[1] - side, 1)
    weight_grad = weight_grad.reshape(pooled.shape[1], layer_grad.shape[1])
    return (weight_grad, new_codes, new_scale, lowest, new_accum)


def solution(mesh):
    mesh = Mesh(mesh.devices.reshape(NX, NZL, NZH, NY, NC), AXES)
    in_specs = (
        P(AXES, None),
        P(AXES, None),
        P(),
        P(AXES, None),
        P(AXES),
        P(SHARD),
        P(SHARD, None),
        P(SHARD),
        P(SHARD),
        P(SHARD),
    )
    out_specs = (P(), P(SHARD, None), P(SHARD), P(SHARD), P(SHARD))
    return jax.shard_map(shards, mesh=mesh, in_specs=in_specs, out_specs=out_specs, check_vma=False)
```

```python
import jax
import jax.numpy as jnp
from jax import lax
from jax.experimental import pallas as pl
from jax.experimental.pallas import tpu as pltpu
from jax.sharding import Mesh, PartitionSpec as P

f32, bf16, i32 = jnp.float32, jnp.bfloat16, jnp.int32
NX, NZL, NZH, NY, NC = 4, 3, 4, 8, 2
AXES = ("x", "zl", "zh", "y", "c")
REP = ("x", "zl")
SHARD = ("zh", "y", "c")
KEYS, EXTRA = 16, 16
NT = (((1,), (1,)), ((), ()))


def dispatch_kernel(here, cap, first_ref, near_ref, w_ref, out_ref, g_ref, slots_ref, aim_ref):
    count, samples = near_ref.shape[0], near_ref.shape[1]
    depth = w_ref.shape[1]
    width = out_ref.shape[2]
    features = w_ref.shape[0] // width
    bags = samples * features
    per_bag = KEYS // features
    group = lax.broadcasted_iota(i32, (here, bags), 0)
    earlier = lax.broadcasted_iota(i32, (bags, bags), 0) < lax.broadcasted_iota(i32, (bags, bags), 1)
    earlier = jnp.where(earlier, 1.0, 0.0).astype(bf16)
    lane = lax.broadcasted_iota(i32, (count * cap, bags), 0)
    packed = jnp.zeros((2 * here, count * cap), f32)
    some = 4
    line = lax.broadcasted_iota(i32, (some * cap, bags), 0)
    for q in range(count):
        lg = near_ref[q, :, :depth]
        for f in range(features):
            block = lax.dot_general(lg, w_ref[f * width : (f + 1) * width, :], NT, preferred_element_type=f32)
            g_ref[f * samples : (f + 1) * samples, :] = block.astype(bf16)
        keys = jnp.transpose(near_ref[q, :, depth:].astype(f32))

        def pick(kind, j):
            at = [kind * KEYS + f * per_bag + j for f in range(features)]
            return jnp.concatenate([keys[i : i + 1, :] for i in at], axis=1)

        owners = [pick(0, j).astype(i32) - first_ref[0] for j in range(per_bag)]
        members = [jnp.where(own == group, 1.0, 0.0) for own in owners]
        stacked = jnp.concatenate(members, axis=0).astype(bf16)
        prefix = jnp.dot(stacked, earlier, preferred_element_type=f32)
        base = jnp.zeros((here, 1), f32)
        for j in range(per_bag):
            member = members[j]
            pos = jnp.sum(member * (prefix[j * here : (j + 1) * here] + base), axis=0, keepdims=True).astype(i32)
            base = base + jnp.sum(member, axis=1, keepdims=True)
            aim_ref[j : j + 1, :] = owners[j] * cap + pos
            place = jnp.where(pos + q * cap == lane, 1.0, 0.0).astype(bf16)
            parts = jnp.concatenate([member * pick(1, j), member * pick(2, j)], axis=0).astype(bf16)
            packed = packed + lax.dot_general(parts, place, NT, preferred_element_type=f32)

        def step(i, carry):
            start = i * some * cap
            aim = aim_ref[:per_bag, :] - start
            hit = aim[0:1, :] == line
            for j in range(1, per_bag):
                hit = hit | (aim[j : j + 1, :] == line)
            chosen = jnp.where(hit, 1.0, 0.0).astype(bf16)
            out = jnp.dot(chosen, g_ref[...], preferred_element_type=f32).astype(bf16)
            for k in range(some):
                out_ref[i * some + k, q * cap : (q + 1) * cap, :] = out[k * cap : (k + 1) * cap]
            return carry

        for i in range(here // some):
            step(i, 0)
    slots_ref[...] = packed
    row = lax.broadcasted_iota(i32, (EXTRA, width), 0)
    for d in range(here):
        extra = jnp.where(row == 0, slots_ref[d : d + 1, :], 0.0)
        extra = jnp.where(row == 1, slots_ref[here + d : here + d + 1, :], extra)
        out_ref[d, count * cap :, :] = extra.astype(bf16)


def vmem():
    return pl.BlockSpec(memory_space=pltpu.VMEM)


def limit():
    return pltpu.CompilerParams(vmem_limit_bytes=40 << 20)


def with_keys(layer_grad, bag_owner, bag_slot):
    samples = layer_grad.shape[0]
    slot = bag_slot.reshape(samples, KEYS) + 1
    keys = jnp.concatenate([bag_owner.reshape(samples, KEYS), slot >> 5, slot & 31], axis=1).astype(bf16)
    return jnp.concatenate([layer_grad, jnp.pad(keys, ((0, 0), (0, 128 - 3 * KEYS)))], axis=1)


def dispatch(first, near, dense_weight, width, here, cap):
    count, samples = near.shape[0], near.shape[1]
    features = dense_weight.shape[0] // width
    return pl.pallas_call(
        lambda *refs: dispatch_kernel(here, cap, *refs),
        out_shape=jax.ShapeDtypeStruct((here, count * cap + EXTRA, width), bf16),
        in_specs=[pl.BlockSpec(memory_space=pltpu.SMEM)] + [vmem()] * 2,
        out_specs=vmem(),
        scratch_shapes=[pltpu.VMEM((samples * features, width), bf16), pltpu.VMEM((2 * here, width), f32), pltpu.VMEM((8, samples * features), i32)],
        compiler_params=limit(),
        name="dispatch",
    )(first, near, dense_weight)


def collect(got, touch):
    here, height, width = got.shape
    many = height - EXTRA
    slots = got[:, many].astype(f32) * 32.0 + got[:, many + 1].astype(f32) - 1.0
    slots = jnp.pad(slots.astype(i32), ((0, 0), (0, EXTRA)), constant_values=-1)
    selector = (jnp.arange(touch, dtype=i32)[:, None] == slots.reshape(1, -1)).astype(bf16)
    return jnp.dot(selector, got.reshape(-1, width), preferred_element_type=f32)


def update_kernel(sums_ref, old_ref, accum_ref, out_ref):
    parts, part, width = sums_ref.shape
    total = sums_ref[0]
    for k in range(1, parts):
        total = total + sums_ref[k]
    new_accum = accum_ref[...] + jnp.mean(total * total, axis=1, keepdims=True)
    updated = old_ref[...] - 0.1 * total / (jnp.sqrt(new_accum) + 1e-06)
    lowest = jnp.min(updated, axis=1, keepdims=True)
    highest = jnp.max(updated, axis=1, keepdims=True)
    new_scale = (highest - lowest) / 255.0
    new_codes = (updated - lowest) / new_scale
    diagonal = lax.broadcasted_iota(i32, (part, part), 0) == lax.broadcasted_iota(i32, (part, part), 1)
    row = lax.broadcasted_iota(i32, (8, part), 0)
    small = jnp.zeros((8, part), f32)
    for i, column in enumerate((new_scale, lowest, new_accum)):
        flat = jnp.sum(jnp.where(diagonal, column, 0.0), axis=0, keepdims=True)
        small = jnp.where(row == i, flat, small)
    small = jnp.concatenate([small, jnp.zeros((8, width - part), f32)], axis=1)
    for k in range(parts):
        out_ref[k, :part, :] = new_codes
        out_ref[k, part:, :] = small


def update(sums, old, old_accum):
    parts, part, width = sums.shape
    return pl.pallas_call(
        update_kernel,
        out_shape=jax.ShapeDtypeStruct((parts, part + 8, width), f32),
        in_specs=[vmem()] * 3,
        out_specs=vmem(),
        compiler_params=limit(),
        name="update",
    )(sums, old, old_accum[:, None])


def swap(a, axis, size, bit):
    return lax.ppermute(a, axis, [(i, i ^ bit) for i in range(size)])


def halve(a, axis, size, bit, dim):
    side = (lax.axis_index(axis) & bit) // bit
    n = a.shape[dim] // 2
    keep = lax.dynamic_slice_in_dim(a, side * n, n, dim)
    send = lax.dynamic_slice_in_dim(a, (1 - side) * n, n, dim)
    return keep + swap(send, axis, size, bit)


def scatter_sum(a, axis, size):
    me = lax.axis_index(axis)
    n = a.shape[0] // size

    def block(k):
        return lax.dynamic_slice_in_dim(a, lax.rem(me + k, size) * n, n, 0)

    got = [shift(block(k), axis, size, k) for k in range(1, size)]
    total = block(0)
    for g in got:
        total = total + g
    return total


def place(pieces, axis, size, dim):
    me = lax.axis_index(axis)
    n = pieces[0].shape[dim]
    out = jnp.concatenate([pieces[0]] * size, axis=dim)
    for k, piece in enumerate(pieces[1:], 1):
        out = lax.dynamic_update_slice_in_dim(out, piece, lax.rem(me - k + size, size) * n, dim)
    return out


def gather(a, axis, size, dim=0):
    return place([a] + [shift(a, axis, size, k) for k in range(1, size)], axis, size, dim)


def shift(a, axis, size, k):
    return lax.ppermute(a, axis, [(i, (i + k) % size) for i in range(size)])


def tie(*arrays):
    return lax.optimization_barrier(arrays)


def double(a, axis, size, bit, dim):
    other = swap(a, axis, size, bit)
    first = (lax.axis_index(axis) & bit) == 0
    return jnp.concatenate([jnp.where(first, a, other), jnp.where(first, other, a)], axis=dim)


def sum_over_three(a):
    me = lax.axis_index("zl")
    got = [a] + [shift(a, "zl", NZL, k) for k in range(1, NZL)]
    total = None
    for source in range(NZL):
        term = got[NZL - 1]
        for k in range(NZL - 1):
            term = jnp.where((me - k) % NZL == source, got[k], term)
        total = term if total is None else total + term
    return total


def shards(pooled, layer_grad, dense_weight, bag_owner, bag_slot, touched, codes, row_scale, row_bias, accum):
    here = NY * NC
    parts = NX * NZL
    width = codes.shape[1]
    touch = touched.shape[0]
    part = touch // parts
    cap = 2 * bag_slot.shape[0] // (NZH * here)
    first = (lax.axis_index("zh") * here).astype(i32).reshape(1)
    near = with_keys(layer_grad, bag_owner, bag_slot)
    columns = jnp.stack(jnp.split(pooled, NZH, axis=1))
    columns = lax.all_to_all(columns, "zh", 0, 0, tiled=True)
    near = lax.all_gather(near, "zh", axis=0, tiled=False)
    near, columns = tie(near, columns)
    rows = dispatch(first, near, dense_weight, width, here, cap)
    rows, near, columns = tie(rows, near, columns)
    got = lax.all_to_all(rows, ("y", "c"), 0, 0, tiled=True)
    lg = near.reshape(-1, near.shape[2])[:, : layer_grad.shape[1]]
    columns = columns.reshape(lg.shape[0], -1)
    w = lax.dot_general(columns, lg, (((0,), (0,)), ((), ())), preferred_element_type=f32)
    w = halve(w, "c", NC, 1, 0)
    w = scatter_sum(w, "x", NX)
    w = gather(sum_over_three(w)[None], "zh", NZH)
    mine = lax.axis_index("x") * NZL + lax.axis_index("zl")
    local = lax.dynamic_slice_in_dim(touched, mine * part, part, 0)
    old = codes[local].astype(f32) * row_scale[local][:, None] + row_bias[local][:, None]
    old_accum = accum[local]
    got, w, old, old_accum = tie(got, w, old, old_accum)

    sums = collect(got, touch).reshape(parts, part, width)
    sums = lax.all_to_all(sums, REP, 0, 0, tiled=True)
    w = halve(w, "y", NY, 1, 0)
    w = w + swap(w, "y", NY, 2)
    w = w + swap(w, "y", NY, 4)
    sums, w = tie(sums, w)

    payload = lax.all_to_all(update(sums, old, old_accum), REP, 0, 0, tiled=True)
    w = double(w, "y", NY, 1, 0)
    pieces = [w] + [shift(w, "x", NX, k) for k in range(1, NX)]
    new_codes = payload[:, :part].reshape(touch, width)
    new_scale, lowest, new_accum = (payload[:, part + i, :part].reshape(touch) for i in range(3))
    pieces[-1], new_codes, new_scale, lowest, new_accum = tie(pieces[-1], new_codes, new_scale, lowest, new_accum)
    w = place(pieces, "x", NX, 1)
    other = swap(w, "c", NC, 1)
    side = lax.axis_index("c") * w.shape[1]
    weight_grad = jnp.concatenate([w, w], axis=1)
    weight_grad = lax.dynamic_update_slice_in_dim(weight_grad, other, w.shape[1] - side, 1)
    weight_grad = weight_grad.reshape(pooled.shape[1], layer_grad.shape[1])
    return (weight_grad, new_codes, new_scale, lowest, new_accum)


def solution(mesh):
    mesh = Mesh(mesh.devices.reshape(NX, NZL, NZH, NY, NC), AXES)
    in_specs = (
        P(AXES, None),
        P(AXES, None),
        P(),
        P(AXES, None),
        P(AXES),
        P(SHARD),
        P(SHARD, None),
        P(SHARD),
        P(SHARD),
        P(SHARD),
    )
    out_specs = (P(), P(SHARD, None), P(SHARD), P(SHARD), P(SHARD))
    return jax.shard_map(shards, mesh=mesh, in_specs=in_specs, out_specs=out_specs, check_vma=False)
```

```python
import jax
import jax.numpy as jnp
from jax import lax
from jax.experimental import pallas as pl
from jax.experimental.pallas import tpu as pltpu
from jax.sharding import Mesh, PartitionSpec as P

f32, bf16, i32 = jnp.float32, jnp.bfloat16, jnp.int32
NX, NZL, NZH, NY, NC = 4, 3, 4, 8, 2
AXES = ("x", "zl", "zh", "y", "c")
REP = ("x", "zl")
SHARD = ("zh", "y", "c")
KEYS, EXTRA = 16, 16
NT = (((1,), (1,)), ((), ()))


def dispatch_kernel(here, cap, first_ref, near_ref, w_ref, out_ref, g_ref, slots_ref, aim_ref):
    count, samples = near_ref.shape[0], near_ref.shape[1]
    depth = w_ref.shape[1]
    width = out_ref.shape[2]
    features = w_ref.shape[0] // width
    bags = samples * features
    per_bag = KEYS // features
    group = lax.broadcasted_iota(i32, (here, bags), 0)
    earlier = lax.broadcasted_iota(i32, (bags, bags), 0) < lax.broadcasted_iota(i32, (bags, bags), 1)
    earlier = jnp.where(earlier, 1.0, 0.0).astype(bf16)
    lane = lax.broadcasted_iota(i32, (count * cap, bags), 0)
    packed = jnp.zeros((2 * here, count * cap), f32)
    some = 4
    line = lax.broadcasted_iota(i32, (some * cap, bags), 0)
    for q in range(count):
        lg = near_ref[q, :, :depth]
        for f in range(features):
            block = lax.dot_general(lg, w_ref[f * width : (f + 1) * width, :], NT, preferred_element_type=f32)
            g_ref[f * samples : (f + 1) * samples, :] = block.astype(bf16)
        keys = jnp.transpose(near_ref[q, :, depth:].astype(f32))

        def pick(kind, j):
            at = [kind * KEYS + f * per_bag + j for f in range(features)]
            return jnp.concatenate([keys[i : i + 1, :] for i in at], axis=1)

        owners = [pick(0, j).astype(i32) - first_ref[0] for j in range(per_bag)]
        members = [jnp.where(own == group, 1.0, 0.0) for own in owners]
        stacked = jnp.concatenate(members, axis=0).astype(bf16)
        prefix = jnp.dot(stacked, earlier, preferred_element_type=f32)
        base = jnp.zeros((here, 1), f32)
        for j in range(per_bag):
            member = members[j]
            pos = jnp.sum(member * (prefix[j * here : (j + 1) * here] + base), axis=0, keepdims=True).astype(i32)
            base = base + jnp.sum(member, axis=1, keepdims=True)
            aim_ref[j : j + 1, :] = owners[j] * cap + pos
            place = jnp.where(pos + q * cap == lane, 1.0, 0.0).astype(bf16)
            parts = jnp.concatenate([member * pick(1, j), member * pick(2, j)], axis=0).astype(bf16)
            packed = packed + lax.dot_general(parts, place, NT, preferred_element_type=f32)

        def step(i, carry):
            start = i * some * cap
            aim = aim_ref[:per_bag, :] - start
            hit = aim[0:1, :] == line
            for j in range(1, per_bag):
                hit = hit | (aim[j : j + 1, :] == line)
            chosen = jnp.where(hit, 1.0, 0.0).astype(bf16)
            out = jnp.dot(chosen, g_ref[...], preferred_element_type=f32).astype(bf16)
            for k in range(some):
                out_ref[i * some + k, q * cap : (q + 1) * cap, :] = out[k * cap : (k + 1) * cap]
            return carry

        for i in range(here // some):
            step(i, 0)
    slots_ref[...] = packed
    row = lax.broadcasted_iota(i32, (EXTRA, width), 0)
    for d in range(here):
        extra = jnp.where(row == 0, slots_ref[d : d + 1, :], 0.0)
        extra = jnp.where(row == 1, slots_ref[here + d : here + d + 1, :], extra)
        out_ref[d, count * cap :, :] = extra.astype(bf16)


def vmem():
    return pl.BlockSpec(memory_space=pltpu.VMEM)


def limit():
    return pltpu.CompilerParams(vmem_limit_bytes=40 << 20)


def with_keys(layer_grad, bag_owner, bag_slot):
    samples = layer_grad.shape[0]
    slot = bag_slot.reshape(samples, KEYS) + 1
    keys = jnp.concatenate([bag_owner.reshape(samples, KEYS), slot >> 5, slot & 31], axis=1).astype(bf16)
    return jnp.concatenate([layer_grad, jnp.pad(keys, ((0, 0), (0, 128 - 3 * KEYS)))], axis=1)


def dispatch(first, near, dense_weight, width, here, cap):
    count, samples = near.shape[0], near.shape[1]
    features = dense_weight.shape[0] // width
    return pl.pallas_call(
        lambda *refs: dispatch_kernel(here, cap, *refs),
        out_shape=jax.ShapeDtypeStruct((here, count * cap + EXTRA, width), bf16),
        in_specs=[pl.BlockSpec(memory_space=pltpu.SMEM)] + [vmem()] * 2,
        out_specs=vmem(),
        scratch_shapes=[pltpu.VMEM((samples * features, width), bf16), pltpu.VMEM((2 * here, width), f32), pltpu.VMEM((8, samples * features), i32)],
        compiler_params=limit(),
        name="dispatch",
    )(first, near, dense_weight)


def collect(got, touch):
    here, height, width = got.shape
    many = height - EXTRA
    slots = got[:, many].astype(f32) * 32.0 + got[:, many + 1].astype(f32) - 1.0
    slots = jnp.pad(slots.astype(i32), ((0, 0), (0, EXTRA)), constant_values=-1)
    selector = (jnp.arange(touch, dtype=i32)[:, None] == slots.reshape(1, -1)).astype(bf16)
    return jnp.dot(selector, got.reshape(-1, width), preferred_element_type=f32)


def update_kernel(sums_ref, old_ref, accum_ref, out_ref):
    parts, part, width = sums_ref.shape
    total = sums_ref[0]
    for k in range(1, parts):
        total = total + sums_ref[k]
    new_accum = accum_ref[...] + jnp.mean(total * total, axis=1, keepdims=True)
    updated = old_ref[...] - 0.1 * total / (jnp.sqrt(new_accum) + 1e-06)
    lowest = jnp.min(updated, axis=1, keepdims=True)
    highest = jnp.max(updated, axis=1, keepdims=True)
    new_scale = (highest - lowest) / 255.0
    new_codes = (updated - lowest) / new_scale
    diagonal = lax.broadcasted_iota(i32, (part, part), 0) == lax.broadcasted_iota(i32, (part, part), 1)
    row = lax.broadcasted_iota(i32, (8, part), 0)
    small = jnp.zeros((8, part), f32)
    for i, column in enumerate((new_scale, lowest, new_accum)):
        flat = jnp.sum(jnp.where(diagonal, column, 0.0), axis=0, keepdims=True)
        small = jnp.where(row == i, flat, small)
    small = jnp.concatenate([small, jnp.zeros((8, width - part), f32)], axis=1)
    for k in range(parts):
        out_ref[k, :part, :] = new_codes
        out_ref[k, part:, :] = small


def update(sums, old, old_accum):
    parts, part, width = sums.shape
    return pl.pallas_call(
        update_kernel,
        out_shape=jax.ShapeDtypeStruct((parts, part + 8, width), f32),
        in_specs=[vmem()] * 3,
        out_specs=vmem(),
        compiler_params=limit(),
        name="update",
    )(sums, old, old_accum[:, None])


def swap(a, axis, size, bit):
    return lax.ppermute(a, axis, [(i, i ^ bit) for i in range(size)])


def halve(a, axis, size, bit, dim):
    side = (lax.axis_index(axis) & bit) // bit
    n = a.shape[dim] // 2
    keep = lax.dynamic_slice_in_dim(a, side * n, n, dim)
    send = lax.dynamic_slice_in_dim(a, (1 - side) * n, n, dim)
    return keep + swap(send, axis, size, bit)


def scatter_sum(a, axis, size):
    me = lax.axis_index(axis)
    n = a.shape[0] // size

    def block(k):
        return lax.dynamic_slice_in_dim(a, lax.rem(me + k, size) * n, n, 0)

    got = [shift(block(k), axis, size, k) for k in range(1, size)]
    total = block(0)
    for g in got:
        total = total + g
    return total


def place(pieces, axis, size, dim):
    me = lax.axis_index(axis)
    n = pieces[0].shape[dim]
    out = jnp.concatenate([pieces[0]] * size, axis=dim)
    for k, piece in enumerate(pieces[1:], 1):
        out = lax.dynamic_update_slice_in_dim(out, piece, lax.rem(me - k + size, size) * n, dim)
    return out


def gather(a, axis, size, dim=0):
    return place([a] + [shift(a, axis, size, k) for k in range(1, size)], axis, size, dim)


def shift(a, axis, size, k):
    return lax.ppermute(a, axis, [(i, (i + k) % size) for i in range(size)])


def tie(*arrays):
    return lax.optimization_barrier(arrays)


def double(a, axis, size, bit, dim):
    other = swap(a, axis, size, bit)
    first = (lax.axis_index(axis) & bit) == 0
    return jnp.concatenate([jnp.where(first, a, other), jnp.where(first, other, a)], axis=dim)


def sum_over_three(a):
    me = lax.axis_index("zl")
    got = [a] + [shift(a, "zl", NZL, k) for k in range(1, NZL)]
    total = None
    for source in range(NZL):
        term = got[NZL - 1]
        for k in range(NZL - 1):
            term = jnp.where((me - k) % NZL == source, got[k], term)
        total = term if total is None else total + term
    return total


def shards(pooled, layer_grad, dense_weight, bag_owner, bag_slot, touched, codes, row_scale, row_bias, accum):
    here = NY * NC
    parts = NX * NZL
    width = codes.shape[1]
    touch = touched.shape[0]
    part = touch // parts
    cap = 2 * bag_slot.shape[0] // (NZH * here)
    first = (lax.axis_index("zh") * here).astype(i32).reshape(1)
    near = with_keys(layer_grad, bag_owner, bag_slot)
    columns = jnp.stack(jnp.split(pooled, NZH, axis=1))
    columns = lax.all_to_all(columns, "zh", 0, 0, tiled=True)
    near = lax.all_gather(near, "zh", axis=0, tiled=False)
    near, columns = tie(near, columns)
    rows = dispatch(first, near, dense_weight, width, here, cap)
    rows, near, columns = tie(rows, near, columns)
    got = lax.all_to_all(rows, ("y", "c"), 0, 0, tiled=True)
    lg = near.reshape(-1, near.shape[2])[:, : layer_grad.shape[1]]
    columns = columns.reshape(lg.shape[0], -1)
    w = lax.dot_general(columns, lg, (((0,), (0,)), ((), ())), preferred_element_type=f32)
    w = halve(w, "c", NC, 1, 0)
    w = scatter_sum(w, "x", NX)
    w = gather(sum_over_three(w)[None], "zh", NZH)
    mine = lax.axis_index("x") * NZL + lax.axis_index("zl")
    local = lax.dynamic_slice_in_dim(touched, mine * part, part, 0)
    old = codes[local].astype(f32) * row_scale[local][:, None] + row_bias[local][:, None]
    old_accum = accum[local]
    got, w, old, old_accum = tie(got, w, old, old_accum)

    sums = collect(got, touch).reshape(parts, part, width)
    sums = lax.all_to_all(sums, REP, 0, 0, tiled=True)
    w = halve(w, "y", NY, 1, 0)
    w = w + swap(w, "y", NY, 2)
    w = w + swap(w, "y", NY, 4)
    sums, w = tie(sums, w)

    payload = lax.all_to_all(update(sums, old, old_accum), REP, 0, 0, tiled=True)
    w = double(w, "y", NY, 1, 0)
    after = shift(w, "x", NX, NX - 1)
    pieces = [w, shift(w, "x", NX, 1), shift(after, "x", NX, NX - 1), after]
    new_codes = payload[:, :part].reshape(touch, width)
    new_scale, lowest, new_accum = (payload[:, part + i, :part].reshape(touch) for i in range(3))
    w = place(pieces, "x", NX, 1)
    other = swap(w, "c", NC, 1)
    other, new_codes, new_scale, lowest, new_accum = tie(other, new_codes, new_scale, lowest, new_accum)
    side = lax.axis_index("c") * w.shape[1]
    weight_grad = jnp.concatenate([w, w], axis=1)
    weight_grad = lax.dynamic_update_slice_in_dim(weight_grad, other, w.shape[1] - side, 1)
    weight_grad = weight_grad.reshape(pooled.shape[1], layer_grad.shape[1])
    return (weight_grad, new_codes, new_scale, lowest, new_accum)


def solution(mesh):
    mesh = Mesh(mesh.devices.reshape(NX, NZL, NZH, NY, NC), AXES)
    in_specs = (
        P(AXES, None),
        P(AXES, None),
        P(),
        P(AXES, None),
        P(AXES),
        P(SHARD),
        P(SHARD, None),
        P(SHARD),
        P(SHARD),
        P(SHARD),
    )
    out_specs = (P(), P(SHARD, None), P(SHARD), P(SHARD), P(SHARD))
    return jax.shard_map(shards, mesh=mesh, in_specs=in_specs, out_specs=out_specs, check_vma=False)
```

```python
import jax
import jax.numpy as jnp
from jax import lax
from jax.experimental import pallas as pl
from jax.experimental.pallas import tpu as pltpu
from jax.sharding import Mesh, PartitionSpec as P

f32, bf16, i32 = jnp.float32, jnp.bfloat16, jnp.int32
NX, NZL, NZH, NY, NC = 4, 3, 4, 8, 2
AXES = ("x", "zl", "zh", "y", "c")
REP = ("x", "zl")
SHARD = ("zh", "y", "c")
KEYS, EXTRA = 16, 16
NT = (((1,), (1,)), ((), ()))


def dispatch_kernel(here, cap, first_ref, near_ref, w_ref, out_ref, g_ref, slots_ref, aim_ref):
    count, samples = near_ref.shape[0], near_ref.shape[1]
    depth = w_ref.shape[1]
    width = out_ref.shape[2]
    features = w_ref.shape[0] // width
    bags = samples * features
    per_bag = KEYS // features
    group = lax.broadcasted_iota(i32, (here, bags), 0)
    earlier = lax.broadcasted_iota(i32, (bags, bags), 0) < lax.broadcasted_iota(i32, (bags, bags), 1)
    earlier = jnp.where(earlier, 1.0, 0.0).astype(bf16)
    lane = lax.broadcasted_iota(i32, (count * cap, bags), 0)
    packed = jnp.zeros((2 * here, count * cap), f32)
    some = 4
    line = lax.broadcasted_iota(i32, (some * cap, bags), 0)
    for q in range(count):
        lg = near_ref[q, :, :depth]
        for f in range(features):
            block = lax.dot_general(lg, w_ref[f * width : (f + 1) * width, :], NT, preferred_element_type=f32)
            g_ref[f * samples : (f + 1) * samples, :] = block.astype(bf16)
        keys = jnp.transpose(near_ref[q, :, depth:].astype(f32))

        def pick(kind, j):
            at = [kind * KEYS + f * per_bag + j for f in range(features)]
            return jnp.concatenate([keys[i : i + 1, :] for i in at], axis=1)

        owners = [pick(0, j).astype(i32) - first_ref[0] for j in range(per_bag)]
        members = [jnp.where(own == group, 1.0, 0.0) for own in owners]
        stacked = jnp.concatenate(members, axis=0).astype(bf16)
        prefix = jnp.dot(stacked, earlier, preferred_element_type=f32)
        base = jnp.zeros((here, 1), f32)
        for j in range(per_bag):
            member = members[j]
            pos = jnp.sum(member * (prefix[j * here : (j + 1) * here] + base), axis=0, keepdims=True).astype(i32)
            base = base + jnp.sum(member, axis=1, keepdims=True)
            aim_ref[j : j + 1, :] = owners[j] * cap + pos
            place = jnp.where(pos + q * cap == lane, 1.0, 0.0).astype(bf16)
            parts = jnp.concatenate([member * pick(1, j), member * pick(2, j)], axis=0).astype(bf16)
            packed = packed + lax.dot_general(parts, place, NT, preferred_element_type=f32)

        def step(i, carry):
            start = i * some * cap
            aim = aim_ref[:per_bag, :] - start
            hit = aim[0:1, :] == line
            for j in range(1, per_bag):
                hit = hit | (aim[j : j + 1, :] == line)
            chosen = jnp.where(hit, 1.0, 0.0).astype(bf16)
            out = jnp.dot(chosen, g_ref[...], preferred_element_type=f32).astype(bf16)
            for k in range(some):
                out_ref[i * some + k, q * cap : (q + 1) * cap, :] = out[k * cap : (k + 1) * cap]
            return carry

        for i in range(here // some):
            step(i, 0)
    slots_ref[...] = packed
    row = lax.broadcasted_iota(i32, (EXTRA, width), 0)
    for d in range(here):
        extra = jnp.where(row == 0, slots_ref[d : d + 1, :], 0.0)
        extra = jnp.where(row == 1, slots_ref[here + d : here + d + 1, :], extra)
        out_ref[d, count * cap :, :] = extra.astype(bf16)


def vmem():
    return pl.BlockSpec(memory_space=pltpu.VMEM)


def limit():
    return pltpu.CompilerParams(vmem_limit_bytes=40 << 20)


def with_keys(layer_grad, bag_owner, bag_slot):
    samples = layer_grad.shape[0]
    slot = bag_slot.reshape(samples, KEYS) + 1
    keys = jnp.concatenate([bag_owner.reshape(samples, KEYS), slot >> 5, slot & 31], axis=1).astype(bf16)
    return jnp.concatenate([layer_grad, jnp.pad(keys, ((0, 0), (0, 128 - 3 * KEYS)))], axis=1)


def dispatch(first, near, dense_weight, width, here, cap):
    count, samples = near.shape[0], near.shape[1]
    features = dense_weight.shape[0] // width
    return pl.pallas_call(
        lambda *refs: dispatch_kernel(here, cap, *refs),
        out_shape=jax.ShapeDtypeStruct((here, count * cap + EXTRA, width), bf16),
        in_specs=[pl.BlockSpec(memory_space=pltpu.SMEM)] + [vmem()] * 2,
        out_specs=vmem(),
        scratch_shapes=[pltpu.VMEM((samples * features, width), bf16), pltpu.VMEM((2 * here, width), f32), pltpu.VMEM((8, samples * features), i32)],
        compiler_params=limit(),
        name="dispatch",
    )(first, near, dense_weight)


def collect(got, touch):
    here, height, width = got.shape
    many = height - EXTRA
    slots = got[:, many].astype(f32) * 32.0 + got[:, many + 1].astype(f32) - 1.0
    slots = jnp.pad(slots.astype(i32), ((0, 0), (0, EXTRA)), constant_values=-1)
    selector = (jnp.arange(touch, dtype=i32)[:, None] == slots.reshape(1, -1)).astype(bf16)
    return jnp.dot(selector, got.reshape(-1, width), preferred_element_type=f32)


def update_kernel(sums_ref, old_ref, accum_ref, out_ref):
    parts, part, width = sums_ref.shape
    total = sums_ref[0]
    for k in range(1, parts):
        total = total + sums_ref[k]
    new_accum = accum_ref[...] + jnp.mean(total * total, axis=1, keepdims=True)
    updated = old_ref[...] - 0.1 * total / (jnp.sqrt(new_accum) + 1e-06)
    lowest = jnp.min(updated, axis=1, keepdims=True)
    highest = jnp.max(updated, axis=1, keepdims=True)
    new_scale = (highest - lowest) / 255.0
    new_codes = (updated - lowest) / new_scale
    diagonal = lax.broadcasted_iota(i32, (part, part), 0) == lax.broadcasted_iota(i32, (part, part), 1)
    row = lax.broadcasted_iota(i32, (8, part), 0)
    small = jnp.zeros((8, part), f32)
    for i, column in enumerate((new_scale, lowest, new_accum)):
        flat = jnp.sum(jnp.where(diagonal, column, 0.0), axis=0, keepdims=True)
        small = jnp.where(row == i, flat, small)
    small = jnp.concatenate([small, jnp.zeros((8, width - part), f32)], axis=1)
    for k in range(parts):
        out_ref[k, :part, :] = new_codes
        out_ref[k, part:, :] = small


def update(sums, old, old_accum):
    parts, part, width = sums.shape
    return pl.pallas_call(
        update_kernel,
        out_shape=jax.ShapeDtypeStruct((parts, part + 8, width), f32),
        in_specs=[vmem()] * 3,
        out_specs=vmem(),
        compiler_params=limit(),
        name="update",
    )(sums, old, old_accum[:, None])


def side_kernel(side_ref, own_ref, other_ref, out_ref):
    n = own_ref.shape[1]
    first = side_ref[0] == 0
    own, other = own_ref[...], other_ref[...]
    out_ref[:, :n, :] = jnp.where(first, own, other)
    out_ref[:, n:, :] = jnp.where(first, other, own)


def side_by_side(side, own, other):
    count, n, columns = own.shape
    half = pl.BlockSpec((1, n, columns), lambda i: (i, 0, 0))
    return pl.pallas_call(
        side_kernel,
        grid=(count,),
        out_shape=jax.ShapeDtypeStruct((count, 2 * n, columns), f32),
        in_specs=[pl.BlockSpec(memory_space=pltpu.SMEM), half, half],
        out_specs=pl.BlockSpec((1, 2 * n, columns), lambda i: (i, 0, 0)),
        name="side_by_side",
    )(side, own, other)


def swap(a, axis, size, bit):
    return lax.ppermute(a, axis, [(i, i ^ bit) for i in range(size)])


def halve(a, axis, size, bit, dim):
    side = (lax.axis_index(axis) & bit) // bit
    n = a.shape[dim] // 2
    keep = lax.dynamic_slice_in_dim(a, side * n, n, dim)
    send = lax.dynamic_slice_in_dim(a, (1 - side) * n, n, dim)
    return keep + swap(send, axis, size, bit)


def scatter_sum(a, axis, size):
    me = lax.axis_index(axis)
    n = a.shape[0] // size

    def block(k):
        return lax.dynamic_slice_in_dim(a, lax.rem(me + k, size) * n, n, 0)

    got = [shift(block(k), axis, size, k) for k in range(1, size)]
    total = block(0)
    for g in got:
        total = total + g
    return total


def place(pieces, axis, size, dim):
    me = lax.axis_index(axis)
    n = pieces[0].shape[dim]
    out = jnp.concatenate([pieces[0]] * size, axis=dim)
    for k, piece in enumerate(pieces[1:], 1):
        out = lax.dynamic_update_slice_in_dim(out, piece, lax.rem(me - k + size, size) * n, dim)
    return out


def gather(a, axis, size, dim=0):
    return place([a] + [shift(a, axis, size, k) for k in range(1, size)], axis, size, dim)


def shift(a, axis, size, k):
    return lax.ppermute(a, axis, [(i, (i + k) % size) for i in range(size)])


def tie(*arrays):
    return lax.optimization_barrier(arrays)


def double(a, axis, size, bit, dim):
    other = swap(a, axis, size, bit)
    first = (lax.axis_index(axis) & bit) == 0
    return jnp.concatenate([jnp.where(first, a, other), jnp.where(first, other, a)], axis=dim)


def sum_over_three(a):
    me = lax.axis_index("zl")
    got = [a] + [shift(a, "zl", NZL, k) for k in range(1, NZL)]
    total = None
    for source in range(NZL):
        term = got[NZL - 1]
        for k in range(NZL - 1):
            term = jnp.where((me - k) % NZL == source, got[k], term)
        total = term if total is None else total + term
    return total


def shards(pooled, layer_grad, dense_weight, bag_owner, bag_slot, touched, codes, row_scale, row_bias, accum):
    here = NY * NC
    parts = NX * NZL
    width = codes.shape[1]
    touch = touched.shape[0]
    part = touch // parts
    cap = 2 * bag_slot.shape[0] // (NZH * here)
    first = (lax.axis_index("zh") * here).astype(i32).reshape(1)
    near = with_keys(layer_grad, bag_owner, bag_slot)
    near = lax.all_gather(near, "zh", axis=0, tiled=False)
    columns = jnp.stack(jnp.split(pooled, NZH, axis=1))
    near, columns = tie(near, columns)
    columns = lax.all_to_all(columns, "zh", 0, 0, tiled=True)
    rows = dispatch(first, near, dense_weight, width, here, cap)
    rows, near, columns = tie(rows, near, columns)
    got = lax.all_to_all(rows, ("y", "c"), 0, 0, tiled=True)
    lg = near.reshape(-1, near.shape[2])[:, : layer_grad.shape[1]]
    columns = columns.reshape(lg.shape[0], -1)
    w = lax.dot_general(columns, lg, (((0,), (0,)), ((), ())), preferred_element_type=f32)
    w = halve(w, "c", NC, 1, 0)
    w = scatter_sum(w, "x", NX)
    w = gather(sum_over_three(w)[None], "zh", NZH)
    mine = lax.axis_index("x") * NZL + lax.axis_index("zl")
    local = lax.dynamic_slice_in_dim(touched, mine * part, part, 0)
    old = codes[local].astype(f32) * row_scale[local][:, None] + row_bias[local][:, None]
    old_accum = accum[local]
    got, w, old, old_accum = tie(got, w, old, old_accum)

    sums = collect(got, touch).reshape(parts, part, width)
    sums = lax.all_to_all(sums, REP, 0, 0, tiled=True)
    w = halve(w, "y", NY, 1, 0)
    w = w + swap(w, "y", NY, 2)
    w = w + swap(w, "y", NY, 4)
    sums, w = tie(sums, w)

    payload = lax.all_to_all(update(sums, old, old_accum), REP, 0, 0, tiled=True)
    w = double(w, "y", NY, 1, 0)
    after = shift(w, "x", NX, NX - 1)
    pieces = [w, shift(w, "x", NX, 1), shift(after, "x", NX, NX - 1), after]
    new_codes = payload[:, :part].reshape(touch, width)
    new_scale, lowest, new_accum = (payload[:, part + i, :part].reshape(touch) for i in range(3))
    w = place(pieces, "x", NX, 1)
    other = swap(w, "c", NC, 1)
    other, new_codes, new_scale, lowest, new_accum = tie(other, new_codes, new_scale, lowest, new_accum)
    weight_grad = side_by_side(lax.axis_index("c").astype(i32).reshape(1), w, other)
    weight_grad = weight_grad.reshape(pooled.shape[1], layer_grad.shape[1])
    return (weight_grad, new_codes, new_scale, lowest, new_accum)


def solution(mesh):
    mesh = Mesh(mesh.devices.reshape(NX, NZL, NZH, NY, NC), AXES)
    in_specs = (
        P(AXES, None),
        P(AXES, None),
        P(),
        P(AXES, None),
        P(AXES),
        P(SHARD),
        P(SHARD, None),
        P(SHARD),
        P(SHARD),
        P(SHARD),
    )
    out_specs = (P(), P(SHARD, None), P(SHARD), P(SHARD), P(SHARD))
    return jax.shard_map(shards, mesh=mesh, in_specs=in_specs, out_specs=out_specs, check_vma=False)
```

```python
import jax
import jax.numpy as jnp
from jax import lax
from jax.experimental import pallas as pl
from jax.experimental.pallas import tpu as pltpu
from jax.sharding import Mesh, PartitionSpec as P

f32, bf16, i32 = jnp.float32, jnp.bfloat16, jnp.int32
NX, NZL, NZH, NY, NC = 4, 3, 4, 8, 2
AXES = ("x", "zl", "zh", "y", "c")
REP = ("x", "zl")
SHARD = ("zh", "y", "c")
KEYS, EXTRA = 16, 16
NT = (((1,), (1,)), ((), ()))


def dispatch_kernel(here, cap, first_ref, near_ref, w_ref, out_ref, g_ref, slots_ref, aim_ref):
    count, samples = near_ref.shape[0], near_ref.shape[1]
    depth = w_ref.shape[1]
    width = out_ref.shape[2]
    features = w_ref.shape[0] // width
    bags = samples * features
    per_bag = KEYS // features
    group = lax.broadcasted_iota(i32, (here, bags), 0)
    earlier = lax.broadcasted_iota(i32, (bags, bags), 0) < lax.broadcasted_iota(i32, (bags, bags), 1)
    earlier = jnp.where(earlier, 1.0, 0.0).astype(bf16)
    lane = lax.broadcasted_iota(i32, (count * cap, bags), 0)
    packed = jnp.zeros((2 * here, count * cap), f32)
    some = 4
    line = lax.broadcasted_iota(i32, (some * cap, bags), 0)
    for q in range(count):
        lg = near_ref[q, :, :depth]
        for f in range(features):
            block = lax.dot_general(lg, w_ref[f * width : (f + 1) * width, :], NT, preferred_element_type=f32)
            g_ref[f * samples : (f + 1) * samples, :] = block.astype(bf16)
        keys = jnp.transpose(near_ref[q, :, depth:].astype(f32))

        def pick(kind, j):
            at = [kind * KEYS + f * per_bag + j for f in range(features)]
            return jnp.concatenate([keys[i : i + 1, :] for i in at], axis=1)

        owners = [pick(0, j).astype(i32) - first_ref[0] for j in range(per_bag)]
        members = [jnp.where(own == group, 1.0, 0.0) for own in owners]
        stacked = jnp.concatenate(members, axis=0).astype(bf16)
        prefix = jnp.dot(stacked, earlier, preferred_element_type=f32)
        base = jnp.zeros((here, 1), f32)
        for j in range(per_bag):
            member = members[j]
            pos = jnp.sum(member * (prefix[j * here : (j + 1) * here] + base), axis=0, keepdims=True).astype(i32)
            base = base + jnp.sum(member, axis=1, keepdims=True)
            aim_ref[j : j + 1, :] = owners[j] * cap + pos
            place = jnp.where(pos + q * cap == lane, 1.0, 0.0).astype(bf16)
            parts = jnp.concatenate([member * pick(1, j), member * pick(2, j)], axis=0).astype(bf16)
            packed = packed + lax.dot_general(parts, place, NT, preferred_element_type=f32)

        def step(i, carry):
            start = i * some * cap
            aim = aim_ref[:per_bag, :] - start
            hit = aim[0:1, :] == line
            for j in range(1, per_bag):
                hit = hit | (aim[j : j + 1, :] == line)
            chosen = jnp.where(hit, 1.0, 0.0).astype(bf16)
            out = jnp.dot(chosen, g_ref[...], preferred_element_type=f32).astype(bf16)
            for k in range(some):
                out_ref[i * some + k, q * cap : (q + 1) * cap, :] = out[k * cap : (k + 1) * cap]
            return carry

        for i in range(here // some):
            step(i, 0)
    slots_ref[...] = packed
    row = lax.broadcasted_iota(i32, (EXTRA, width), 0)
    for d in range(here):
        extra = jnp.where(row == 0, slots_ref[d : d + 1, :], 0.0)
        extra = jnp.where(row == 1, slots_ref[here + d : here + d + 1, :], extra)
        out_ref[d, count * cap :, :] = extra.astype(bf16)


def vmem():
    return pl.BlockSpec(memory_space=pltpu.VMEM)


def limit():
    return pltpu.CompilerParams(vmem_limit_bytes=40 << 20)


def with_keys(layer_grad, bag_owner, bag_slot):
    samples = layer_grad.shape[0]
    slot = bag_slot.reshape(samples, KEYS) + 1
    keys = jnp.concatenate([bag_owner.reshape(samples, KEYS), slot >> 5, slot & 31], axis=1).astype(bf16)
    return jnp.concatenate([layer_grad, jnp.pad(keys, ((0, 0), (0, 128 - 3 * KEYS)))], axis=1)


def dispatch(first, near, dense_weight, width, here, cap):
    count, samples = near.shape[0], near.shape[1]
    features = dense_weight.shape[0] // width
    return pl.pallas_call(
        lambda *refs: dispatch_kernel(here, cap, *refs),
        out_shape=jax.ShapeDtypeStruct((here, count * cap + EXTRA, width), bf16),
        in_specs=[pl.BlockSpec(memory_space=pltpu.SMEM)] + [vmem()] * 2,
        out_specs=vmem(),
        scratch_shapes=[pltpu.VMEM((samples * features, width), bf16), pltpu.VMEM((2 * here, width), f32), pltpu.VMEM((8, samples * features), i32)],
        compiler_params=limit(),
        name="dispatch",
    )(first, near, dense_weight)


def collect(got, touch):
    here, height, width = got.shape
    many = height - EXTRA
    slots = got[:, many].astype(f32) * 32.0 + got[:, many + 1].astype(f32) - 1.0
    slots = jnp.pad(slots.astype(i32), ((0, 0), (0, EXTRA)), constant_values=-1)
    selector = (jnp.arange(touch, dtype=i32)[:, None] == slots.reshape(1, -1)).astype(bf16)
    return jnp.dot(selector, got.reshape(-1, width), preferred_element_type=f32)


def update_kernel(sums_ref, old_ref, accum_ref, out_ref):
    parts, part, width = sums_ref.shape
    total = sums_ref[0]
    for k in range(1, parts):
        total = total + sums_ref[k]
    new_accum = accum_ref[...] + jnp.mean(total * total, axis=1, keepdims=True)
    updated = old_ref[...] - 0.1 * total / (jnp.sqrt(new_accum) + 1e-06)
    lowest = jnp.min(updated, axis=1, keepdims=True)
    highest = jnp.max(updated, axis=1, keepdims=True)
    new_scale = (highest - lowest) / 255.0
    new_codes = (updated - lowest) / new_scale
    diagonal = lax.broadcasted_iota(i32, (part, part), 0) == lax.broadcasted_iota(i32, (part, part), 1)
    row = lax.broadcasted_iota(i32, (8, part), 0)
    small = jnp.zeros((8, part), f32)
    for i, column in enumerate((new_scale, lowest, new_accum)):
        flat = jnp.sum(jnp.where(diagonal, column, 0.0), axis=0, keepdims=True)
        small = jnp.where(row == i, flat, small)
    small = jnp.concatenate([small, jnp.zeros((8, width - part), f32)], axis=1)
    for k in range(parts):
        out_ref[k, :part, :] = new_codes
        out_ref[k, part:, :] = small


def update(sums, old, old_accum):
    parts, part, width = sums.shape
    return pl.pallas_call(
        update_kernel,
        out_shape=jax.ShapeDtypeStruct((parts, part + 8, width), f32),
        in_specs=[vmem()] * 3,
        out_specs=vmem(),
        compiler_params=limit(),
        name="update",
    )(sums, old, old_accum[:, None])


def side_kernel(side_ref, own_ref, other_ref, out_ref):
    n = own_ref.shape[1]
    first = side_ref[0] == 0
    own, other = own_ref[...], other_ref[...]
    out_ref[:, :n, :] = jnp.where(first, own, other)
    out_ref[:, n:, :] = jnp.where(first, other, own)


def side_by_side(side, own, other):
    count, n, columns = own.shape
    half = pl.BlockSpec((1, n, columns), lambda i: (i, 0, 0))
    return pl.pallas_call(
        side_kernel,
        grid=(count,),
        out_shape=jax.ShapeDtypeStruct((count, 2 * n, columns), f32),
        in_specs=[pl.BlockSpec(memory_space=pltpu.SMEM), half, half],
        out_specs=pl.BlockSpec((1, 2 * n, columns), lambda i: (i, 0, 0)),
        name="side_by_side",
    )(side, own, other)


def swap(a, axis, size, bit):
    return lax.ppermute(a, axis, [(i, i ^ bit) for i in range(size)])


def halve(a, axis, size, bit, dim):
    side = (lax.axis_index(axis) & bit) // bit
    n = a.shape[dim] // 2
    keep = lax.dynamic_slice_in_dim(a, side * n, n, dim)
    send = lax.dynamic_slice_in_dim(a, (1 - side) * n, n, dim)
    return keep + swap(send, axis, size, bit)


def scatter_sum(a, axis, size):
    me = lax.axis_index(axis)
    n = a.shape[0] // size

    def block(k):
        return lax.dynamic_slice_in_dim(a, lax.rem(me + k, size) * n, n, 0)

    got = [shift(block(k), axis, size, k) for k in range(1, size)]
    total = block(0)
    for g in got:
        total = total + g
    return total


def place(pieces, axis, size, dim):
    me = lax.axis_index(axis)
    n = pieces[0].shape[dim]
    out = jnp.concatenate([pieces[0]] * size, axis=dim)
    for k, piece in enumerate(pieces[1:], 1):
        out = lax.dynamic_update_slice_in_dim(out, piece, lax.rem(me - k + size, size) * n, dim)
    return out


def gather(a, axis, size, dim=0):
    return place([a] + [shift(a, axis, size, k) for k in range(1, size)], axis, size, dim)


def shift(a, axis, size, k):
    return lax.ppermute(a, axis, [(i, (i + k) % size) for i in range(size)])


def tie(*arrays):
    return lax.optimization_barrier(arrays)


def double(a, axis, size, bit, dim):
    other = swap(a, axis, size, bit)
    first = (lax.axis_index(axis) & bit) == 0
    return jnp.concatenate([jnp.where(first, a, other), jnp.where(first, other, a)], axis=dim)


def sum_over_three(a):
    me = lax.axis_index("zl")
    got = [a] + [shift(a, "zl", NZL, k) for k in range(1, NZL)]
    total = None
    for source in range(NZL):
        term = got[NZL - 1]
        for k in range(NZL - 1):
            term = jnp.where((me - k) % NZL == source, got[k], term)
        total = term if total is None else total + term
    return total


def shards(pooled, layer_grad, dense_weight, bag_owner, bag_slot, touched, codes, row_scale, row_bias, accum):
    here = NY * NC
    parts = NX * NZL
    width = codes.shape[1]
    touch = touched.shape[0]
    part = touch // parts
    cap = 2 * bag_slot.shape[0] // (NZH * here)
    first = (lax.axis_index("zh") * here).astype(i32).reshape(1)
    near = with_keys(layer_grad, bag_owner, bag_slot)
    near = lax.all_gather(near, "zh", axis=0, tiled=False)
    columns = jnp.stack(jnp.split(pooled, NZH, axis=1))
    near, columns = tie(near, columns)
    columns = lax.all_to_all(columns, "zh", 0, 0, tiled=True)
    rows = dispatch(first, near, dense_weight, width, here, cap)
    rows, near = tie(rows, near)
    got = lax.all_to_all(rows, ("y", "c"), 0, 0, tiled=True)
    lg = near.reshape(-1, near.shape[2])[:, : layer_grad.shape[1]]
    columns = columns.reshape(lg.shape[0], -1)
    w = lax.dot_general(columns, lg, (((0,), (0,)), ((), ())), preferred_element_type=f32)
    w = halve(w, "c", NC, 1, 0)
    w = scatter_sum(w, "x", NX)
    w = gather(sum_over_three(w)[None], "zh", NZH)
    mine = lax.axis_index("x") * NZL + lax.axis_index("zl")
    local = lax.dynamic_slice_in_dim(touched, mine * part, part, 0)
    old = codes[local].astype(f32) * row_scale[local][:, None] + row_bias[local][:, None]
    old_accum = accum[local]
    got, w, old, old_accum = tie(got, w, old, old_accum)

    sums = collect(got, touch).reshape(parts, part, width)
    sums = lax.all_to_all(sums, REP, 0, 0, tiled=True)
    w = halve(w, "y", NY, 1, 0)
    w = w + swap(w, "y", NY, 2)
    w = w + swap(w, "y", NY, 4)
    sums, w = tie(sums, w)

    payload = lax.all_to_all(update(sums, old, old_accum), REP, 0, 0, tiled=True)
    w = double(w, "y", NY, 1, 0)
    after = shift(w, "x", NX, NX - 1)
    pieces = [w, shift(w, "x", NX, 1), shift(after, "x", NX, NX - 1), after]
    new_codes = payload[:, :part].reshape(touch, width)
    new_scale, lowest, new_accum = (payload[:, part + i, :part].reshape(touch) for i in range(3))
    w = place(pieces, "x", NX, 1)
    other = swap(w, "c", NC, 1)
    other, new_codes, new_scale, lowest, new_accum = tie(other, new_codes, new_scale, lowest, new_accum)
    weight_grad = side_by_side(lax.axis_index("c").astype(i32).reshape(1), w, other)
    weight_grad = weight_grad.reshape(pooled.shape[1], layer_grad.shape[1])
    return (weight_grad, new_codes, new_scale, lowest, new_accum)


def solution(mesh):
    mesh = Mesh(mesh.devices.reshape(NX, NZL, NZH, NY, NC), AXES)
    in_specs = (
        P(AXES, None),
        P(AXES, None),
        P(),
        P(AXES, None),
        P(AXES),
        P(SHARD),
        P(SHARD, None),
        P(SHARD),
        P(SHARD),
        P(SHARD),
    )
    out_specs = (P(), P(SHARD, None), P(SHARD), P(SHARD), P(SHARD))
    return jax.shard_map(shards, mesh=mesh, in_specs=in_specs, out_specs=out_specs, check_vma=False)
```
